256 devices in a mesh: seq: 32 (over x, z), head: 8 (over y, core).
Axes of the slice: x: 4, y: 4, z: 8, core: 2. Of those that a mesh axis runs over, the one named last changes fastest.
Arguments:
- inputs: bfloat16 [16384, 2048], P('seq'), may hold values from -11 to 11
- out_grad: bfloat16 [16384, 2048], P('seq'), may hold values from -6 to 6
- w_query: bfloat16 [2048, 1024], P(None, 'head'), may hold values from -1 to 1
- w_key: bfloat16 [2048, 512], P(None, 'head'), may hold values from -1 to 1
- w_value: bfloat16 [2048, 512], P(None, 'head'), may hold values from -0.125 to 0.125
- w_output: bfloat16 [1024, 2048], P('head'), may hold values from -0.1875 to 0.1875
Outputs:
- grad_inputs: bfloat16 [16384, 2048], P('seq', 'head')
- grad_query: float32 [2048, 1024], P('seq', 'head')
- grad_key: float32 [2048, 512], P('seq', 'head')
- grad_value: float32 [2048, 512], P('seq', 'head')
- grad_output: float32 [1024, 2048], P('head', 'seq')
The draws below stay inside these ranges and needn't reach their ends.
All inputs are finite; a program needn't handle non-finite values.
Results may differ from the reference program's by a relative error of at most 0.04.
Values may be sent and summed in bfloat16 or wider, within the bound.
A program may use at most 64 MiB of HBM per device.

```python
import math
import jax
import jax.numpy as jnp
from jax import lax

D = 2048
HQ = 16
HK = 8
HD = 64
TOKENS = 16384


def draw_inputs(key, part):
    key = jax.random.fold_in(key, 11)
    first_key = jax.random.fold_in(key, 0)
    return jnp.clip(jax.random.normal(first_key, (TOKENS, D), jnp.float32), -6.0, 6.0).astype(jnp.bfloat16)


def draw_w_query(key, part):
    key = jax.random.fold_in(key, 23)
    noise_part = jax.random.normal(key, (D, HK, HQ // HK, HD), jnp.float32) / math.sqrt(D)
    return jnp.clip(noise_part, -0.9, 0.9).reshape(D, HQ * HD).astype(jnp.bfloat16)


def draw_w_key(key, part):
    key = jax.random.fold_in(key, 37)
    noise_part = jax.random.normal(key, (D, HK, 1, HD), jnp.float32) / math.sqrt(D)
    return jnp.clip(noise_part, -0.9, 0.9).reshape(D, HK * HD).astype(jnp.bfloat16)


def spiked(drawn, key, source, target, parts, factor):
    owner, partner = [(jnp.arange(drawn.shape[dim]) // (drawn.shape[dim] // parts)).reshape([-1 if axis == dim else 1 for axis in range(drawn.ndim)]) for dim in (source, target)]
    chosen = jax.random.permutation(key, parts)[partner]
    strong = (owner == chosen) | (owner == (partner + parts // 2) % parts)
    return jnp.where(strong, factor * drawn, drawn)


def levels(stream_key, shape, cuts, low, high):
    def one(axis_at, blocks):
        steps = jax.random.uniform(jax.random.fold_in(jax.random.fold_in(stream_key, 6), axis_at), (blocks,), jnp.float32, low / len(cuts), high / len(cuts))
        return jnp.repeat(jnp.exp(steps), shape[axis_at] // blocks).reshape((-1,) + (1,) * (len(shape) - axis_at - 1))

    factor_of = one(*cuts[0])
    for cut in cuts[1:]:
        factor_of = factor_of * one(*cut)
    return factor_of


def bell_draw(key, extent, spread, reach, cuts=(), kind=jnp.bfloat16):
    factor_of = levels(key, extent, cuts, -0.22, 0.18) if cuts else 1.0
    array = jax.random.normal(key, extent, jnp.float32) * spread * factor_of
    return jnp.minimum(jnp.maximum(array, -reach), reach).astype(kind)


def gaussian_with(stream_key, shape, spread, most, cuts, heavy, kind=jnp.bfloat16):
    entries = spread * jax.random.normal(stream_key, shape, jnp.float32)
    if cuts:
        entries = entries * levels(stream_key, shape, cuts, -0.22, 0.18)
    return jnp.clip(spiked(entries, jax.random.fold_in(stream_key, 3), *heavy), -most, most).astype(kind)


def setup_inputs(seed: int = 0) -> dict:
    seeds = jax.random.split(jax.random.key(seed), 7)
    inputs = draw_inputs(jax.random.fold_in(seeds[6], 71), 0)
    out_grad = gaussian_with(seeds[1], (TOKENS, D), 1.0, 6.0, ((0, 32),), (0, 1, 32, 2.75))
    w_query = draw_w_query(jax.random.fold_in(seeds[6], 71), 0)
    w_key = draw_w_key(jax.random.fold_in(seeds[6], 71), 0)
    w_value = bell_draw(seeds[4], (D, HK * HD), D ** -0.5, 0.125, ((1, 8),))
    w_output = bell_draw(seeds[5], (HQ * HD, D), (HQ * HD) ** -0.5, 0.1875, ((0, 8),))
    return dict(inputs=inputs, out_grad=out_grad, w_query=w_query, w_key=w_key, w_value=w_value, w_output=w_output)


ROPE_BASE = 500000.0


def rotary(positions):
    half_dim = HD // 2
    frequency = ROPE_BASE ** (-(jnp.arange(half_dim, dtype=jnp.float32) * 2.0 / HD))
    angles = positions[:, None] * frequency[None, :]
    return jnp.cos(angles), jnp.sin(angles)


def rotate(vectors, cos_table, sin_table):
    half_dim = vectors.shape[-1] // 2
    front_half, back_half = vectors[..., :half_dim], vectors[..., half_dim:]
    return jnp.concatenate([front_half * cos_table - back_half * sin_table, back_half * cos_table + front_half * sin_table], -1)


def unrotate(vectors, cos_table, sin_table):
    half_dim = vectors.shape[-1] // 2
    front_half, back_half = vectors[..., :half_dim], vectors[..., half_dim:]
    return jnp.concatenate([front_half * cos_table + back_half * sin_table, back_half * cos_table - front_half * sin_table], -1)


def reference(inputs, out_grad, w_query, w_key, w_value, w_output):
    group_size = HQ // HK
    scale_factor = HD ** -0.5
    positions = jnp.arange(TOKENS).astype(jnp.float32)
    cos_table, sin_table = rotary(positions)
    cos_heads, sin_heads = cos_table[:, None, :], sin_table[:, None, :]
    queries = rotate(jnp.dot(inputs, w_query, preferred_element_type=jnp.float32).reshape(TOKENS, HQ, HD), cos_heads, sin_heads).astype(jnp.bfloat16)
    key_rows = rotate(jnp.dot(inputs, w_key, preferred_element_type=jnp.float32).reshape(TOKENS, HK, HD), cos_heads, sin_heads).astype(jnp.bfloat16)
    value_rows = jnp.dot(inputs, w_value, preferred_element_type=jnp.float32).astype(jnp.bfloat16).reshape(TOKENS, HK, HD)
    grad_heads = jnp.dot(out_grad, w_output.T, preferred_element_type=jnp.float32).astype(jnp.bfloat16).reshape(TOKENS, HQ, HD)
    position_ids = jnp.arange(TOKENS)
    causal = position_ids[:, None] >= position_ids[None, :]
    query_heads = jnp.transpose(queries, (1, 0, 2))
    key_heads = jnp.transpose(jnp.repeat(key_rows, group_size, axis=1), (1, 0, 2))
    value_heads = jnp.transpose(jnp.repeat(value_rows, group_size, axis=1), (1, 0, 2))
    dout_heads = jnp.transpose(grad_heads, (1, 0, 2))

    def single_head(head_items):
        query_one, key_one, value_one, dout_one = head_items
        scores = jnp.dot(query_one, key_one.T, preferred_element_type=jnp.float32) * scale_factor
        scores = jnp.where(causal, scores, -jnp.inf)
        row_max = jnp.max(scores, axis=-1)
        log_total = row_max + jnp.log(jnp.sum(jnp.exp(scores - row_max[:, None]), axis=-1))
        probability = jnp.exp(scores - log_total[:, None])
        prob_low = probability.astype(jnp.bfloat16)
        attn_out = jnp.dot(prob_low, value_one, preferred_element_type=jnp.float32).astype(jnp.bfloat16)
        delta_sum = jnp.sum(dout_one.astype(jnp.float32) * attn_out.astype(jnp.float32), axis=-1)
        dprob_full = jnp.dot(dout_one, value_one.T, preferred_element_type=jnp.float32)
        dscore = (probability * (dprob_full - delta_sum[:, None])).astype(jnp.bfloat16)
        dq_raw = jnp.dot(dscore, key_one, preferred_element_type=jnp.float32) * scale_factor
        dk_raw = jnp.dot(dscore.T, query_one, preferred_element_type=jnp.float32) * scale_factor
        dv_raw = jnp.dot(prob_low.T, dout_one, preferred_element_type=jnp.float32)
        return attn_out, dq_raw, dk_raw, dv_raw

    attn_out, dq_raw, dk_raw, dv_raw = lax.map(single_head, (query_heads, key_heads, value_heads, dout_heads))
    out_rows = jnp.transpose(attn_out, (1, 0, 2)).reshape(TOKENS, HQ * HD)
    dq_rows = unrotate(jnp.transpose(dq_raw, (1, 0, 2)), cos_heads, sin_heads).astype(jnp.bfloat16).reshape(TOKENS, HQ * HD)
    dk_sum = jnp.transpose(dk_raw.reshape(HK, group_size, TOKENS, HD).sum(axis=1), (1, 0, 2))
    dv_sum = jnp.transpose(dv_raw.reshape(HK, group_size, TOKENS, HD).sum(axis=1), (1, 0, 2))
    dk_rows = unrotate(dk_sum, cos_heads, sin_heads).astype(jnp.bfloat16).reshape(TOKENS, HK * HD)
    dv_rows = dv_sum.astype(jnp.bfloat16).reshape(TOKENS, HK * HD)
    grad_query = jnp.dot(inputs.T, dq_rows, preferred_element_type=jnp.float32)
    grad_key = jnp.dot(inputs.T, dk_rows, preferred_element_type=jnp.float32)
    grad_value = jnp.dot(inputs.T, dv_rows, preferred_element_type=jnp.float32)
    grad_output = jnp.dot(out_rows.T, out_grad, preferred_element_type=jnp.float32)
    summed = jnp.dot(dq_rows, w_query.T, preferred_element_type=jnp.float32)
    summed = summed + jnp.dot(dk_rows, w_key.T, preferred_element_type=jnp.float32)
    summed = summed + jnp.dot(dv_rows, w_value.T, preferred_element_type=jnp.float32)
    return summed.astype(jnp.bfloat16), grad_query, grad_key, grad_value, grad_output
```

```python
import functools

import jax
import jax.numpy as jnp
from jax import lax
from jax.experimental import pallas as pl
from jax.experimental.pallas import tpu as pltpu
from jax.sharding import PartitionSpec as P

HD = 64
NX, NZ, NH = 4, 8, 8
ROPE_BASE = 500000.0
NEG = -1e30
F32, BF16 = jnp.float32, jnp.bfloat16
MESH = pl.DeviceIdType.MESH


def rotary(positions):
    half_dim = HD // 2
    frequency = ROPE_BASE ** (-(jnp.arange(half_dim, dtype=jnp.float32) * 2.0 / HD))
    angles = positions[:, None] * frequency[None, :]
    return jnp.cos(angles), jnp.sin(angles)


def mod(value, size):
    return lax.rem(value + 2 * size, size)


class Links:
    def __init__(self, send_sems, recv_sems):
        self.send_sems, self.recv_sems = send_sems, recv_sems
        self.used, self.open = 0, []

    def send(self, src, dst, device):
        index = self.used
        self.used += 1
        copy = pltpu.make_async_remote_copy(
            src_ref=src,
            dst_ref=dst,
            send_sem=self.send_sems.at[index],
            recv_sem=self.recv_sems.at[index],
            device_id=device,
            device_id_type=MESH,
        )
        copy.start()
        self.open.append(copy)
        return index

    def arrived(self, index, landing):
        pltpu.make_async_copy(landing, landing, self.recv_sems.at[index]).wait()

    def drain(self):
        for copy in self.open:
            copy.wait_send()
        self.open = []


def together(*streams):
    streams = list(streams)
    while streams:
        for stream in list(streams):
            try:
                next(stream)
            except StopIteration:
                streams.remove(stream)


def gather_ring(links, slots, own, where, size, right, left, cut):
    far = size // 2
    low, high = cut
    held_r, held_l = own, own
    for step in range(1, far + 1):
        slot_r, slot_l = mod(where - step + 1, size), mod(where + step - 1, size)
        if step == far:
            held_r, held_l = low(held_r), high(held_l)
            place_r, place_l = low(slots(slot_r)), high(slots(slot_l))
        else:
            place_r, place_l = slots(slot_r), slots(slot_l)
        got_r = links.send(held_r, place_r, right)
        got_l = links.send(held_l, place_l, left)
        yield
        held_r, held_l = slots(mod(where - step, size)), slots(mod(where + step, size))
        if step == far:
            links.arrived(got_r, low(held_r))
            links.arrived(got_l, high(held_l))
        else:
            links.arrived(got_r, held_r)
            links.arrived(got_l, held_l)


def scatter_ring(links, mine, snd, from_left, from_right, where, size, right, left, cut, finish):
    far = size // 2
    low, high = cut
    owner = mod(where + far, size)
    snd(owner)[...] = mine(owner)[...].astype(BF16)
    got_r = links.send(low(snd(owner)), low(from_left(0)), right)
    got_l = links.send(high(snd(owner)), high(from_right(0)), left)
    for step in range(2, far + 1):
        yield
        for got, came, place, sign, part, target in (
            (got_r, from_left, from_left, 1, low, right),
            (got_l, from_right, from_right, -1, high, left),
        ):
            owner = mod(where + sign * (far - step + 1), size)
            if step == 2:
                links.arrived(got, part(came(0)))
                other = high if part is low else low
                part(snd(owner))[...] = (
                    part(mine(owner))[...].astype(F32) + part(came(0))[...].astype(F32)
                ).astype(BF16)
                other(snd(owner))[...] = other(mine(owner))[...].astype(BF16)
            else:
                links.arrived(got, came(step - 2))
                snd(owner)[...] = (
                    mine(owner)[...].astype(F32) + came(step - 2)[...].astype(F32)
                ).astype(BF16)
            sent = links.send(snd(owner), place(step - 1), target)
            if sign == 1:
                got_r = sent
            else:
                got_l = sent
    yield
    links.arrived(got_r, from_left(far - 1))
    links.arrived(got_l, from_right(far - 1))
    finish(
        mine(where)[...].astype(F32)
        + from_left(far - 1)[...].astype(F32)
        + from_right(far - 1)[...].astype(F32)
    )


def seq_place():
    me = lax.axis_index("seq")
    return lax.div(me, NZ), lax.rem(me, NZ)


def seq_dev(x, z):
    return {"seq": x * NZ + z}


def greet(devices):
    barrier = pltpu.get_barrier_semaphore()
    for device in devices:
        pl.semaphore_signal(barrier, inc=1, device_id=device, device_id_type=MESH)
    pl.semaphore_wait(barrier, len(devices))


def nn(a, b):
    return lax.dot_general(a, b, (((1,), (0,)), ((), ())), preferred_element_type=F32)


def nt(a, b):
    return lax.dot_general(a, b, (((1,), (1,)), ((), ())), preferred_element_type=F32)


def attention_kernel(
    qd_own, kv_own, w_own,
    od_out, dkv_out, w_all,
    qd, kv, kvt, scores, probs, stats, o_sum, dq_sum, dkv,
    od, od_l, od_r, od_back, od_land, dkv_snd, dkv_l, dkv_r, dkv_back, dkv_land,
    send_sems, recv_sems, copy_sems,
):
    x, z = seq_place()
    head = lax.axis_index("head")
    chunk = kv_own.shape[1]
    lanes = qd_own.shape[2]
    right_x, left_x = seq_dev(mod(x + 1, NX), z), seq_dev(mod(x - 1, NX), z)
    across_x, mirror_x = seq_dev(mod(x + 2, NX), z), seq_dev(NX - 1 - x, z)
    right_z, left_z = seq_dev(x, mod(z + 1, NZ)), seq_dev(x, mod(z - 1, NZ))
    mirror_z = seq_dev(x, NZ - 1 - z)
    others = [{"head": mod(head + step, NH)} for step in range(1, NH)]
    greet([right_x, left_x, across_x, mirror_x, right_z, left_z, mirror_z] + others)
    links = Links(send_sems, recv_sems)

    sent = links.send(qd_own.at[1], qd.at[x, 1], mirror_z)
    sent_kv = links.send(kv_own.at[1], kv.at[z, 1], mirror_x)
    local = [
        pltpu.make_async_copy(qd_own.at[0], qd.at[x, 0], copy_sems.at[0]),
        pltpu.make_async_copy(kv_own.at[0], kv.at[z, 0], copy_sems.at[1]),
        pltpu.make_async_copy(w_own.at[head], w_all.at[head], copy_sems.at[2]),
    ]
    for copy in local:
        copy.start()
    rows_q = (lambda ref: ref.at[0:64], lambda ref: ref.at[64:128])
    rows_k = (lambda ref: ref.at[0 : chunk // 2], lambda ref: ref.at[chunk // 2 : chunk])

    def mirrored(index, landing, ring):
        yield
        links.arrived(index, landing)
        yield from ring

    together(
        gather_ring(links, lambda i: qd.at[i, 0], qd_own.at[0], x, NX, right_x, left_x, rows_q),
        gather_ring(links, lambda i: kv.at[i, 0], kv_own.at[0], z, NZ, right_z, left_z, rows_k),
        mirrored(sent, qd.at[x, 1],
                 gather_ring(links, lambda i: qd.at[i, 1], qd.at[x, 1], x, NX, right_x, left_x, rows_q)),
        mirrored(sent_kv, kv.at[z, 1],
                 gather_ring(links, lambda i: kv.at[i, 1], kv.at[z, 1], z, NZ, right_z, left_z, rows_k)),
    )
    for copy in local:
        copy.wait()
    weights = [
        (links.send(w_own.at[mod(head + step, NH)], w_all.at[head], others[step - 1]), step)
        for step in range(1, NH)
    ]

    def flip(index, _):
        i, a = lax.div(index, 2), lax.rem(index, 2)
        kvt[i, a] = kv[i, a].astype(F32).T.astype(BF16)
        dkv[i, a] = jnp.zeros(dkv.shape[2:], F32)
        return 0

    lax.fori_loop(0, 2 * NZ, flip, 0)

    def extents(group):
        i, a = lax.div(group, 2), lax.rem(group, 2)
        first = a == 0
        block = NZ * i + jnp.where(first, z, NZ - 1 - z)
        diag = jnp.where(first, (i == x).astype(jnp.int32), (i == NX - 1 - x).astype(jnp.int32))
        count_a = jnp.clip(block - NZ * x + 1, 0, NZ)
        count_b = jnp.clip(block - NZ * (NX - 1 - x) + a, 0, NZ)
        full_a = count_a - jnp.where(first, diag, 0)
        full_b = count_b - jnp.where(first, 0, diag)
        return i, a, full_a, full_a + full_b, diag

    def tile(k, full_a):
        in_a = k < full_a
        return jnp.where(in_a, k, k - full_a), jnp.where(in_a, 0, 1)

    def fold(values, op):
        return op(values.reshape(chunk // 8, 8, lanes), axis=0)

    def forward(group, offset):
        i, a, full_a, full, diag = extents(group)
        diag_z = jnp.where(a == 0, z, NZ - 1 - z)
        q_only = jnp.concatenate([qd[i, a, 0:64, :], jnp.zeros((64, lanes), BF16)], 0)

        def score(k, top):
            zc, ac = tile(k, full_a)
            s = nn(kv[zc, ac], q_only)
            scores[k] = s
            return jnp.maximum(top, fold(s, jnp.max))

        top = lax.fori_loop(0, full, score, jnp.full((8, lanes), NEG, F32))

        def score_diag(top):
            s = nn(kv[diag_z, a], q_only)
            key = lax.broadcasted_iota(jnp.int32, (chunk, lanes), 0)
            row = lax.rem(lax.broadcasted_iota(jnp.int32, (chunk, lanes), 1), chunk)
            s = jnp.where(row >= key, s, NEG)
            scores[full] = s
            return jnp.maximum(top, fold(s, jnp.max))

        top = lax.cond(diag == 1, score_diag, lambda t: t, top)
        top = jnp.max(top, axis=0, keepdims=True)
        o_sum[group] = jnp.zeros((64, lanes), F32)

        def weigh(k, total):
            zc, ac = tile(k, full_a)
            zc = jnp.where(k == full, diag_z, zc)
            ac = jnp.where(k == full, a, ac)
            p = jnp.exp(scores[k] - top)
            low = p.astype(BF16)
            probs[offset + k] = low
            o_sum[group] += nn(kvt[zc, ac, 64:128, :], low)
            return total + fold(p, jnp.sum)

        total = lax.fori_loop(0, full + diag, weigh, jnp.zeros((8, lanes), F32))
        dot_do = jnp.sum(o_sum[group] * qd[i, a, 64:128, :].astype(F32), axis=0, keepdims=True)
        stats[x, 0, pl.ds(group, 1), :] = top
        stats[x, 1, pl.ds(group, 1), :] = jnp.sum(total, axis=0, keepdims=True)
        stats[x, 2, pl.ds(group, 1), :] = dot_do
        return offset + full + diag

    lax.fori_loop(0, 2 * NX, forward, 0)

    shares = [
        (links.send(stats.at[x], stats.at[x], device), mod(x - step, NX))
        for step, device in ((1, right_x), (2, across_x), (3, left_x))
    ]
    for index, source in shares:
        links.arrived(index, stats.at[source])

    def backward(group, offset):
        i, a, full_a, full, diag = extents(group)
        diag_z = jnp.where(a == 0, z, NZ - 1 - z)
        tops = [stats[n, 0, pl.ds(group, 1), :] for n in range(NX)]
        top = functools.reduce(jnp.maximum, tops)
        weights_of = [jnp.exp(t - top) for t in tops]
        total = sum(stats[n, 1, pl.ds(group, 1), :] * weights_of[n] for n in range(NX))
        inverse = 1.0 / total
        delta = sum(stats[n, 2, pl.ds(group, 1), :] * weights_of[n] for n in range(NX)) * inverse
        scale = jnp.exp(stats[x, 0, pl.ds(group, 1), :] - top) * inverse
        blank = jnp.zeros((64, lanes), BF16)
        do = qd[i, a, 64:128, :]
        do_only = jnp.concatenate([blank, do], 0)
        q_scaled = jnp.concatenate([(qd[i, a, 0:64, :].astype(F32) * scale).astype(BF16), blank], 0)
        do_scaled = jnp.concatenate([blank, (do.astype(F32) * scale).astype(BF16)], 0)
        dq_sum[...] = jnp.zeros((64, lanes), F32)

        def step(k, _):
            zc, ac = tile(k, full_a)
            zc = jnp.where(k == full, diag_z, zc)
            ac = jnp.where(k == full, a, ac)
            p = probs[offset + k]
            dp = nn(kv[zc, ac], do_only)
            ds = (p.astype(F32) * (dp - delta)).astype(BF16)
            dkv[zc, ac] += nt(ds, q_scaled) + nt(p, do_scaled)
            dq_sum[...] += nn(kvt[zc, ac, 0:64, :], ds)
            return 0

        lax.fori_loop(0, full + diag, step, 0)
        od[i, a, 0:64, :] = (o_sum[group] * scale).astype(BF16)
        od[i, a, 64:128, :] = (dq_sum[...] * (scale * 0.125)).astype(BF16)
        return offset + full + diag

    lax.fori_loop(0, 2 * NX, backward, 0)

    pair_q = (lambda ref: ref.at[:, 0:64], lambda ref: ref.at[:, 64:128])
    pair_k = (lambda ref: ref.at[:, 0 : chunk // 2], lambda ref: ref.at[:, chunk // 2 : chunk])

    def finish_od(value):
        od_out[0] = value[0].astype(BF16)
        od_back[...] = value[1].astype(BF16)

    def finish_dkv(value):
        dkv_out[0] = value[0]
        dkv_back[...] = value[1].astype(BF16)

    together(
        scatter_ring(links, lambda i: od.at[i], lambda i: od.at[i], lambda i: od_l.at[i], lambda i: od_r.at[i],
                     x, NX, right_x, left_x, pair_q, finish_od),
        scatter_ring(links, lambda i: dkv.at[i], lambda i: dkv_snd.at[i], lambda i: dkv_l.at[i],
                     lambda i: dkv_r.at[i], z, NZ, right_z, left_z, pair_k, finish_dkv),
    )
    got_od = links.send(od_back, od_land, mirror_z)
    got_dkv = links.send(dkv_back, dkv_land, mirror_x)
    links.arrived(got_od, od_land)
    links.arrived(got_dkv, dkv_land)
    od_out[1] = od_land[...]
    dkv_out[1] = dkv_land[...].astype(F32)
    for index, step in weights:
        links.arrived(index, w_all.at[mod(head - step, NH)])
    links.drain()


def attention(qd_own, kv_own, w_own):
    chunk, lanes = kv_own.shape[1], qd_own.shape[2]
    tiles = (2 * NX * 2 * NZ) // 2 + 1
    vmem = pl.BlockSpec(memory_space=pltpu.VMEM)
    anywhere = pl.BlockSpec(memory_space=pl.ANY)
    copies = 56
    return pl.pallas_call(
        attention_kernel,
        out_shape=(
            jax.ShapeDtypeStruct((2, 128, lanes), BF16),
            jax.ShapeDtypeStruct((2, chunk, 128), F32),
            jax.ShapeDtypeStruct(w_own.shape, BF16),
        ),
        in_specs=[vmem, vmem, anywhere],
        out_specs=(vmem, vmem, anywhere),
        scratch_shapes=[
            pltpu.VMEM((NX, 2, 128, lanes), BF16),
            pltpu.VMEM((NZ, 2, chunk, 128), BF16),
            pltpu.VMEM((NZ, 2, 128, chunk), BF16),
            pltpu.VMEM((2 * NZ, chunk, lanes), F32),
            pltpu.VMEM((tiles, chunk, lanes), BF16),
            pltpu.VMEM((NX, 3, 8, lanes), F32),
            pltpu.VMEM((2 * NX, 64, lanes), F32),
            pltpu.VMEM((64, lanes), F32),
            pltpu.VMEM((NZ, 2, chunk, 128), F32),
            pltpu.VMEM((NX, 2, 128, lanes), BF16),
            pltpu.VMEM((NX // 2, 2, 128, lanes), BF16),
            pltpu.VMEM((NX // 2, 2, 128, lanes), BF16),
            pltpu.VMEM((128, lanes), BF16),
            pltpu.VMEM((128, lanes), BF16),
            pltpu.VMEM((NZ, 2, chunk, 128), BF16),
            pltpu.VMEM((NZ // 2, 2, chunk, 128), BF16),
            pltpu.VMEM((NZ // 2, 2, chunk, 128), BF16),
            pltpu.VMEM((chunk, 128), BF16),
            pltpu.VMEM((chunk, 128), BF16),
            pltpu.SemaphoreType.DMA((copies,)),
            pltpu.SemaphoreType.DMA((copies,)),
            pltpu.SemaphoreType.DMA((3,)),
        ],
        compiler_params=pltpu.CompilerParams(
            collective_id=0, has_side_effects=True, vmem_limit_bytes=56 * 1024 * 1024
        ),
        name="attention",
    )(qd_own, kv_own, w_own)


def finish_kernel(
    g_own, proj, outp,
    g_all, proj_out, outp_out,
    proj_snd, proj_l, proj_r, proj_z, projz_snd, projz_l, projz_r,
    outp_snd, outp_l, outp_r, outp_x, outpx_snd, outpx_l, outpx_r,
    send_sems, recv_sems, copy_sem,
):
    x, z = seq_place()
    head = lax.axis_index("head")
    y, core = lax.div(head, 2), lax.rem(head, 2)
    right_x, left_x = seq_dev(mod(x + 1, NX), z), seq_dev(mod(x - 1, NX), z)
    right_z, left_z = seq_dev(x, mod(z + 1, NZ)), seq_dev(x, mod(z - 1, NZ))
    right_y, left_y = {"head": mod(y + 1, 4) * 2 + core}, {"head": mod(y - 1, 4) * 2 + core}
    twin = {"head": y * 2 + 1 - core}
    greet([right_x, left_x, right_z, left_z, right_y, left_y, twin])
    links = Links(send_sems, recv_sems)
    keep = pltpu.make_async_copy(g_own, g_all.at[head], copy_sem)
    keep.start()

    def slot(i, c):
        return g_all.at[i * 2 + c]

    def spread():
        rows = g_own.shape[0] // 2
        cut = (lambda ref: ref.at[0:rows], lambda ref: ref.at[rows : 2 * rows])
        ring = gather_ring(links, lambda i: slot(i, core), g_own, y, 4, right_y, left_y, cut)
        next(ring)
        got = [(links.send(g_own, slot(y, core), twin), y)]
        yield
        next(ring)
        for i in (mod(y - 1, 4), mod(y + 1, 4)):
            got.append((links.send(slot(i, core), slot(i, core), twin), i))
        yield
        for _ in ring:
            pass
        i = mod(y + 2, 4)
        got.append((links.send(slot(i, core), slot(i, core), twin), i))
        yield
        for index, i in got:
            links.arrived(index, slot(i, 1 - core))

    def halves(dim, size):
        low, high = slice(0, size // 2), slice(size // 2, size)
        if dim == 0:
            return (lambda ref: ref.at[low], lambda ref: ref.at[high])
        return (lambda ref: ref.at[:, low], lambda ref: ref.at[:, high])

    slab = proj.shape[2]

    def keep_to(ref):
        def write(value):
            ref[...] = value.astype(ref.dtype)

        return write

    def proj_sums():
        yield from scatter_ring(
            links, lambda i: proj.at[i], lambda i: proj_snd.at[i], lambda i: proj_l.at[i], lambda i: proj_r.at[i],
            x, NX, right_x, left_x, halves(0, NZ), keep_to(proj_z))
        yield from scatter_ring(
            links, lambda i: proj_z.at[i], lambda i: projz_snd.at[i], lambda i: projz_l.at[i], lambda i: projz_r.at[i],
            z, NZ, right_z, left_z, halves(0, slab), keep_to(proj_out))

    def outp_sums():
        yield from scatter_ring(
            links, lambda i: outp.at[:, i], lambda i: outp_snd.at[i], lambda i: outp_l.at[i], lambda i: outp_r.at[i],
            z, NZ, right_z, left_z, halves(0, NX), keep_to(outp_x))
        yield from scatter_ring(
            links, lambda i: outp_x.at[i], lambda i: outpx_snd.at[i], lambda i: outpx_l.at[i], lambda i: outpx_r.at[i],
            x, NX, right_x, left_x, halves(0, slab), keep_to(outp_out))

    together(proj_sums(), outp_sums(), spread())
    keep.wait()
    links.drain()


def finish(g_own, proj, outp):
    vmem = pl.BlockSpec(memory_space=pltpu.VMEM)
    _, _, slab, wide = proj.shape
    narrow = outp.shape[3]
    copies = 48

    def vm(*shape, dtype=BF16):
        return pltpu.VMEM(shape, dtype)

    return pl.pallas_call(
        finish_kernel,
        out_shape=(
            jax.ShapeDtypeStruct((NH,) + g_own.shape, BF16),
            jax.ShapeDtypeStruct((slab, wide), F32),
            jax.ShapeDtypeStruct((slab, narrow), F32),
        ),
        in_specs=[vmem] * 3,
        out_specs=(vmem,) * 3,
        scratch_shapes=[
            vm(NX, NZ, slab, wide), vm(NX // 2, NZ, slab, wide), vm(NX // 2, NZ, slab, wide),
            vm(NZ, slab, wide, dtype=F32), vm(NZ, slab, wide), vm(NZ // 2, slab, wide), vm(NZ // 2, slab, wide),
            vm(NZ, NX, slab, narrow), vm(NZ // 2, NX, slab, narrow), vm(NZ // 2, NX, slab, narrow),
            vm(NX, slab, narrow, dtype=F32), vm(NX, slab, narrow), vm(NX // 2, slab, narrow), vm(NX // 2, slab, narrow),
            pltpu.SemaphoreType.DMA((copies,)),
            pltpu.SemaphoreType.DMA((copies,)),
            pltpu.SemaphoreType.DMA,
        ],
        compiler_params=pltpu.CompilerParams(
            collective_id=1, has_side_effects=True, vmem_limit_bytes=40 * 1024 * 1024
        ),
        name="finish",
    )(g_own, proj, outp)


def body(inputs, out_grad, w_query, w_key, w_value, w_output):
    tokens = inputs.shape[0]
    chunk = tokens // 2
    model = inputs.shape[1]
    me = lax.axis_index("seq")
    positions = (me * tokens + jnp.arange(tokens, dtype=jnp.int32)).astype(F32)
    cos, sin = rotary(positions)
    cos_t, sin_t = cos.T, sin.T

    q = jnp.einsum("td,df->ft", inputs, w_query, preferred_element_type=F32).reshape(2, HD, tokens)
    front, back = q[:, :32], q[:, 32:]
    q = jnp.concatenate([front * cos_t - back * sin_t, back * cos_t + front * sin_t], 1).astype(BF16)
    q = q * jnp.asarray(0.125, BF16)
    do = jnp.einsum("td,fd->ft", out_grad, w_output, preferred_element_type=F32).astype(BF16)
    qd = jnp.concatenate([q, do.reshape(2, HD, tokens)], 1)
    qd = qd.reshape(2, 128, 2, chunk).transpose(2, 1, 0, 3).reshape(2, 128, 2 * chunk)
    k = jnp.dot(inputs, w_key, preferred_element_type=F32)
    front, back = k[:, :32], k[:, 32:]
    k = jnp.concatenate([front * cos - back * sin, back * cos + front * sin], 1)
    v = jnp.dot(inputs, w_value, preferred_element_type=F32)
    kv = jnp.concatenate([k, v], 1).astype(BF16).reshape(2, chunk, 128)
    w_own = jnp.concatenate([w_query, w_key, w_value], 1).reshape(NH, model // NH, 256)

    od, dkv, w_all = attention(qd, kv, w_own)

    od = od.reshape(2, 2, HD, 2, chunk)
    od = od.transpose(1, 3, 2, 0, 4).reshape(2, 2, HD, tokens)
    o = od[0].reshape(128, tokens)
    dq = od[1].astype(F32)
    front, back = dq[:, :32], dq[:, 32:]
    dq = jnp.concatenate([front * cos_t + back * sin_t, back * cos_t - front * sin_t], 1)
    dq = dq.astype(BF16).reshape(128, tokens).T
    dkv = dkv.reshape(tokens, 128)
    front, back = dkv[:, :32], dkv[:, 32:64]
    g = jnp.concatenate(
        [
            dq,
            (front * cos + back * sin).astype(BF16),
            (back * cos - front * sin).astype(BF16),
            dkv[:, 64:].astype(BF16),
        ],
        1,
    )
    slab = model // (NX * NZ)
    proj = jnp.einsum("tc,tf->cf", inputs, g, preferred_element_type=F32).astype(BF16)
    outp = jnp.einsum("tc,ft->cf", out_grad, o, preferred_element_type=F32).astype(BF16)
    g_all, proj_sum, outp_sum = finish(
        g, proj.reshape(NX, NZ, slab, 256), outp.reshape(NX, NZ, slab, 128)
    )
    grad_inputs = jnp.einsum("htf,hcf->tc", g_all, w_all, preferred_element_type=F32).astype(BF16)
    return grad_inputs, proj_sum[:, :128], proj_sum[:, 128:192], proj_sum[:, 192:], outp_sum.T


def solution(mesh):
    placed = (
        P("seq", None),
        P("seq", None),
        P(None, "head"),
        P(None, "head"),
        P(None, "head"),
        P("head", None),
    )
    return jax.shard_map(
        body,
        mesh=mesh,
        in_specs=placed,
        out_specs=(
            P("seq", "head"),
            P("seq", "head"),
            P("seq", "head"),
            P("seq", "head"),
            P("head", "seq"),
        ),
        check_vma=False,
    )
```

```python
import functools

import jax
import jax.numpy as jnp
from jax import lax
from jax.experimental import pallas as pl
from jax.experimental.pallas import tpu as pltpu
from jax.sharding import PartitionSpec as P

HD = 64
NX, NZ, NH = 4, 8, 8
ROPE_BASE = 500000.0
NEG = -1e30
F32, BF16 = jnp.float32, jnp.bfloat16
MESH = pl.DeviceIdType.MESH


def rotary(positions):
    half_dim = HD // 2
    frequency = ROPE_BASE ** (-(jnp.arange(half_dim, dtype=jnp.float32) * 2.0 / HD))
    angles = positions[:, None] * frequency[None, :]
    return jnp.cos(angles), jnp.sin(angles)


def mod(value, size):
    return lax.rem(value + 2 * size, size)


class Links:
    def __init__(self, send_sems, recv_sems):
        self.send_sems, self.recv_sems = send_sems, recv_sems
        self.used, self.open = 0, []

    def send(self, src, dst, device):
        index = self.used
        self.used += 1
        copy = pltpu.make_async_remote_copy(
            src_ref=src,
            dst_ref=dst,
            send_sem=self.send_sems.at[index],
            recv_sem=self.recv_sems.at[index],
            device_id=device,
            device_id_type=MESH,
        )
        copy.start()
        self.open.append(copy)
        return index

    def arrived(self, index, landing):
        pltpu.make_async_copy(landing, landing, self.recv_sems.at[index]).wait()

    def drain(self):
        for copy in self.open:
            copy.wait_send()
        self.open = []


def together(*streams):
    streams = list(streams)
    while streams:
        for stream in list(streams):
            try:
                next(stream)
            except StopIteration:
                streams.remove(stream)


def gather_ring(links, slots, own, where, size, right, left, cut):
    far = size // 2
    low, high = cut
    held_r, held_l = own, own
    for step in range(1, far + 1):
        slot_r, slot_l = mod(where - step + 1, size), mod(where + step - 1, size)
        if step == far:
            held_r, held_l = low(held_r), high(held_l)
            place_r, place_l = low(slots(slot_r)), high(slots(slot_l))
        else:
            place_r, place_l = slots(slot_r), slots(slot_l)
        got_r = links.send(held_r, place_r, right)
        got_l = links.send(held_l, place_l, left)
        yield
        held_r, held_l = slots(mod(where - step, size)), slots(mod(where + step, size))
        if step == far:
            links.arrived(got_r, low(held_r))
            links.arrived(got_l, high(held_l))
        else:
            links.arrived(got_r, held_r)
            links.arrived(got_l, held_l)


def scatter_ring(links, mine, snd, from_left, from_right, where, size, right, left, cut, finish):
    far = size // 2
    low, high = cut
    owner = mod(where + far, size)
    snd(owner)[...] = mine(owner)[...].astype(BF16)
    got_r = links.send(low(snd(owner)), low(from_left(0)), right)
    got_l = links.send(high(snd(owner)), high(from_right(0)), left)
    for step in range(2, far + 1):
        yield
        for got, came, place, sign, part, target in (
            (got_r, from_left, from_left, 1, low, right),
            (got_l, from_right, from_right, -1, high, left),
        ):
            owner = mod(where + sign * (far - step + 1), size)
            if step == 2:
                links.arrived(got, part(came(0)))
                other = high if part is low else low
                part(snd(owner))[...] = (
                    part(mine(owner))[...].astype(F32) + part(came(0))[...].astype(F32)
                ).astype(BF16)
                other(snd(owner))[...] = other(mine(owner))[...].astype(BF16)
            else:
                links.arrived(got, came(step - 2))
                snd(owner)[...] = (
                    mine(owner)[...].astype(F32) + came(step - 2)[...].astype(F32)
                ).astype(BF16)
            sent = links.send(snd(owner), place(step - 1), target)
            if sign == 1:
                got_r = sent
            else:
                got_l = sent
    yield
    links.arrived(got_r, from_left(far - 1))
    links.arrived(got_l, from_right(far - 1))
    finish(
        mine(where)[...].astype(F32)
        + from_left(far - 1)[...].astype(F32)
        + from_right(far - 1)[...].astype(F32)
    )


def seq_place():
    me = lax.axis_index("seq")
    return lax.div(me, NZ), lax.rem(me, NZ)


def seq_dev(x, z):
    return {"seq": x * NZ + z}


def greet(devices):
    barrier = pltpu.get_barrier_semaphore()
    for device in devices:
        pl.semaphore_signal(barrier, inc=1, device_id=device, device_id_type=MESH)
    pl.semaphore_wait(barrier, len(devices))


def nn(a, b):
    return lax.dot_general(a, b, (((1,), (0,)), ((), ())), preferred_element_type=F32)


def nt(a, b):
    return lax.dot_general(a, b, (((1,), (1,)), ((), ())), preferred_element_type=F32)


def fold(values, op):
    return op(values.reshape(values.shape[0] // 8, 8, values.shape[1]), axis=0)


def attention_kernel(
    q_own, do_own, kv_own, wq_own, wkv_own,
    o_out, dq_out, dkv_out, wq_all, wkv_all,
    qg, dg, kv, kvt, both, probs, tops, stats, lse, delta, o_sum, dq_sum, dkv,
    ring_o, o_l, o_r, o_back, o_land, ring_q, q_l, q_r, q_back, q_land,
    dkv_snd, dkv_l, dkv_r, dkv_back, dkv_land,
    send_sems, recv_sems, copy_sems,
):
    x, z = seq_place()
    head = lax.axis_index("head")
    chunk, lanes = kv_own.shape[1], q_own.shape[2]
    far_x, far_z = NX - 1 - x, NZ - 1 - z
    right_x, left_x = seq_dev(mod(x + 1, NX), z), seq_dev(mod(x - 1, NX), z)
    across_x, mirror_x = seq_dev(mod(x + 2, NX), z), seq_dev(far_x, z)
    right_z, left_z = seq_dev(x, mod(z + 1, NZ)), seq_dev(x, mod(z - 1, NZ))
    mirror_z = seq_dev(x, far_z)
    others = [{"head": mod(head + step, NH)} for step in range(1, NH)]
    greet([right_x, left_x, across_x, mirror_x, right_z, left_z, mirror_z] + others)
    links = Links(send_sems, recv_sems)

    sent_q = links.send(q_own.at[1], qg.at[x, 1], mirror_z)
    sent_kv = links.send(kv_own.at[1], kv.at[z, 1], mirror_x)
    local = [
        pltpu.make_async_copy(q_own.at[0], qg.at[x, 0], copy_sems.at[0]),
        pltpu.make_async_copy(kv_own.at[0], kv.at[z, 0], copy_sems.at[1]),
        pltpu.make_async_copy(do_own.at[0], dg.at[x, 0], copy_sems.at[2]),
        pltpu.make_async_copy(wq_own.at[head], wq_all.at[head], copy_sems.at[3]),
        pltpu.make_async_copy(wkv_own.at[head], wkv_all.at[head], copy_sems.at[4]),
    ]
    for copy in local:
        copy.start()
    rows_q = (lambda ref: ref.at[0:32], lambda ref: ref.at[32:64])
    rows_k = (lambda ref: ref.at[0 : chunk // 2], lambda ref: ref.at[chunk // 2 : chunk])

    def ring_x(ref, a, own):
        return gather_ring(links, lambda i: ref.at[i, a], own, x, NX, right_x, left_x, rows_q)

    def ring_z(a, own):
        return gather_ring(links, lambda i: kv.at[i, a], own, z, NZ, right_z, left_z, rows_k)

    def pump(*rings):
        for ring in rings:
            next(ring, None)

    q_a, k_a = ring_x(qg, 0, q_own.at[0]), ring_z(0, kv_own.at[0])
    q_b, k_b = ring_x(qg, 1, qg.at[x, 1]), ring_z(1, kv.at[z, 1])
    d_a, d_b = ring_x(dg, 0, do_own.at[0]), ring_x(dg, 1, dg.at[x, 1])
    pump(q_a, k_a)
    links.arrived(sent_q, qg.at[x, 1])
    pump(q_b)
    links.arrived(sent_kv, kv.at[z, 1])
    pump(k_b)
    sent_do = links.send(do_own.at[1], dg.at[x, 1], mirror_z)
    dkv[...] = jnp.zeros(dkv.shape, F32)
    o_sum[...] = jnp.zeros(o_sum.shape, F32)
    dq_sum[...] = jnp.zeros(dq_sum.shape, F32)
    both[...] = jnp.zeros(both.shape, BF16)
    stats[x, 0] = jnp.full(stats.shape[2:], NEG, F32)
    stats[x, 1] = jnp.zeros(stats.shape[2:], F32)
    for copy in local:
        copy.wait()
    pump(q_a, k_a, q_b, k_b, d_a)
    links.arrived(sent_do, dg.at[x, 1])
    pump(d_b)
    pump(q_a, q_b)

    def full_tiles(zc):
        tiles = []
        for n in range(3):
            first = n < far_x
            half, block = jnp.where(first, 0, 1), jnp.where(first, x + 1 + n, n + 1)
            tiles += [(half, block, a, zc * 6 + n * 2 + a) for a in range(2)]
        return tiles

    def cross_tiles(zc, a):
        base = 6 * NZ + (0 if a == 0 else 2 * z + 1) + 2 * zc
        return [(0, x, a, base), (1, far_x, a, base + 1)]

    def forward(zc, tiles, cut=()):
        found = []
        for n, (half, block, a, place) in enumerate(tiles):
            s = nn(kv[zc, half][:, 0:64], qg[block, a])
            if n in cut:
                key = lax.broadcasted_iota(jnp.int32, (chunk, lanes), 0)
                row = lax.rem(lax.broadcasted_iota(jnp.int32, (chunk, lanes), 1), chunk)
                on_diagonal = zc == (z if a == 0 else far_z)
                s = jnp.where(row - key >= jnp.where(on_diagonal, 0, -chunk), s, NEG)
            found.append(s)
        highs = [jnp.max(fold(s, jnp.max), axis=0, keepdims=True) for s in found]
        raised = [jnp.exp(s - high) for s, high in zip(found, highs)]
        lows = [p.astype(BF16) for p in raised]
        totals = [jnp.sum(fold(p, jnp.sum), axis=0, keepdims=True) for p in raised]
        for (_, _, _, place), low, high in zip(tiles, lows, highs):
            probs[place] = low
            tops[pl.ds(place, 1), :] = high
        outs = [nn(kvt[zc, half, 64:128, :], low) for (half, _, _, _), low in zip(tiles, lows)]
        for (_, block, a, _), high, total, out in zip(tiles, highs, totals, outs):
            group = pl.ds(block * 2 + a, 1)
            old = stats[x, 0, group, :]
            top = jnp.maximum(old, high)
            keep, add = jnp.exp(old - top), jnp.exp(high - top)
            stats[x, 0, group, :] = top
            stats[x, 1, group, :] = stats[x, 1, group, :] * keep + total * add
            o_sum[block, a] = o_sum[block, a] * keep + out * add

    def forward_slot(zc):
        for half in range(2):
            kvt[zc, half] = kv[zc, half].astype(F32).T.astype(BF16)
        forward(zc, full_tiles(zc))
        pl.when(zc < z)(lambda: forward(zc, cross_tiles(zc, 0)))
        pl.when(zc == z)(lambda: forward(zc, cross_tiles(zc, 0)[:1], (0,)))
        pl.when(zc <= far_z)(lambda: forward(zc, cross_tiles(zc, 1), (1,)))

    def slots(work, distances):
        def one(n, _):
            work(mod(z + distances[0] + n * (distances[-1] - distances[0]), NZ))
            return 0

        lax.fori_loop(0, len(distances), one, 0)

    slots(forward_slot, (0,))
    pump(k_a, k_b, d_a, d_b)
    slots(forward_slot, (1, -1))
    pump(k_a, k_b, d_a, d_b)
    slots(forward_slot, (2, -2))
    pump(k_a, k_b)
    slots(forward_slot, (3, -3))
    slots(forward_slot, (4,))

    weights = []
    for step in range(1, NH):
        there = mod(head + step, NH)
        for own, whole in ((wq_own, wq_all), (wkv_own, wkv_all)):
            weights.append((links.send(own.at[there], whole.at[head], others[step - 1]), whole, step))

    for block in range(NX):
        for a in range(2):
            group = block * 2 + a
            stats[x, 2, group : group + 1, :] = jnp.sum(
                o_sum[block, a] * dg[block, a].astype(F32), axis=0, keepdims=True
            )
    shares = [
        (links.send(stats.at[x], stats.at[x], device), mod(x - step, NX))
        for step, device in ((1, right_x), (2, across_x), (3, left_x))
    ]
    for block in range(NX):
        for a in range(2):
            both[block, 0:64, a * lanes : (a + 1) * lanes] = qg[block, a]
            both[block, 64:128, (2 + a) * lanes : (3 + a) * lanes] = dg[block, a]
    for index, source in shares:
        links.arrived(index, stats.at[source])
    top = functools.reduce(jnp.maximum, [stats[n, 0] for n in range(NX)])
    part = [jnp.exp(stats[n, 0] - top) for n in range(NX)]
    total = sum(stats[n, 1] * part[n] for n in range(NX))
    lse[...] = top + jnp.log(total)
    delta[...] = sum(stats[n, 2] * part[n] for n in range(NX)) / total
    share = jnp.exp(stats[x, 0] - lse[...])
    for block in range(NX):
        for a in range(2):
            group = block * 2 + a
            ring_o[block, a] = (o_sum[block, a] * share[group : group + 1]).astype(BF16)

    def backward_tile(zc, half, block, a, place):
        group = pl.ds(block * 2 + a, 1)
        scale = jnp.exp(tops[pl.ds(place, 1), :] - lse[group, :])
        p = probs[place] * scale.astype(BF16)
        dp = nn(kv[zc, half], both[block, :, (2 + a) * lanes : (3 + a) * lanes])
        return p, p * (dp - delta[group, :]).astype(BF16)

    def backward_full(zc):
        tiles = full_tiles(zc)
        done = [backward_tile(zc, *tile) for tile in tiles]
        for (half, block, a, _), (_, ds) in zip(tiles, done):
            dq_sum[block, a] += nn(kvt[zc, half, 0:64, :], ds)
        for n in range(3):
            half, block = tiles[2 * n][:2]
            (p0, ds0), (p1, ds1) = done[2 * n], done[2 * n + 1]
            dkv[zc, half] += nt(jnp.concatenate([ds0, ds1, p0, p1], 1), both[block])

    def backward_some(zc, tiles):
        done = [backward_tile(zc, *tile) for tile in tiles]
        for (half, block, a, _), (p, ds) in zip(tiles, done):
            dq_sum[block, a] += nn(kvt[zc, half, 0:64, :], ds)
            dkv[zc, half] += nt(ds, both[block, :, a * lanes : (a + 1) * lanes]) + nt(
                p, both[block, :, (2 + a) * lanes : (3 + a) * lanes]
            )

    def backward_slot(zc):
        backward_full(zc)
        pl.when(zc < z)(lambda: backward_some(zc, cross_tiles(zc, 0)))
        pl.when(zc == z)(lambda: backward_some(zc, cross_tiles(zc, 0)[:1]))
        pl.when(zc <= far_z)(lambda: backward_some(zc, cross_tiles(zc, 1)))

    pair_q = (lambda ref: ref.at[:, 0:32], lambda ref: ref.at[:, 32:64])
    pair_k = (lambda ref: ref.at[:, 0 : chunk // 2], lambda ref: ref.at[:, chunk // 2 : chunk])
    backs = {}

    def finish_to(name, out, back, land, device):
        def write(value):
            out[0] = value[0].astype(out.dtype)
            back[...] = value[1].astype(BF16)
            backs[name] = (links.send(back, land, device), out, land)

        return write

    def sums_x(ring, from_l, from_r, done):
        return scatter_ring(links, lambda i: ring.at[i], lambda i: ring.at[i], lambda i: from_l.at[i],
                            lambda i: from_r.at[i], x, NX, right_x, left_x, pair_q, done)

    o_ring = sums_x(ring_o, o_l, o_r, finish_to("o", o_out, o_back, o_land, mirror_z))
    q_ring = sums_x(ring_q, q_l, q_r, finish_to("q", dq_out, q_back, q_land, mirror_z))
    kv_ring = scatter_ring(links, lambda i: dkv.at[i], lambda i: dkv_snd.at[i], lambda i: dkv_l.at[i],
                           lambda i: dkv_r.at[i], z, NZ, right_z, left_z, pair_k,
                           finish_to("kv", dkv_out, dkv_back, dkv_land, mirror_x))
    pump(o_ring)
    slots(backward_slot, (4,))
    pump(kv_ring, o_ring)
    slots(backward_slot, (3, -3))
    pump(kv_ring, o_ring)
    slots(backward_slot, (2, -2))
    pump(kv_ring)
    slots(backward_slot, (1, -1))
    pump(kv_ring)
    slots(backward_slot, (0,))
    for block in range(NX):
        for a in range(2):
            group = block * 2 + a
            ring_q[block, a] = (dq_sum[block, a] * 0.125).astype(BF16)
    pump(q_ring)
    pump(kv_ring)
    pump(q_ring)
    pump(q_ring)
    for index, out, land in backs.values():
        links.arrived(index, land)
        out[1] = land[...].astype(out.dtype)
    for index, whole, step in weights:
        links.arrived(index, whole.at[mod(head - step, NH)])
    links.drain()


def attention(q_own, do_own, kv_own, wq_own, wkv_own):
    chunk, lanes = kv_own.shape[1], q_own.shape[2]
    tiles = (2 * NX * 2 * NZ) // 2 + 1
    vmem = pl.BlockSpec(memory_space=pltpu.VMEM)
    anywhere = pl.BlockSpec(memory_space=pl.ANY)
    copies = 80

    def vm(*shape, dtype=BF16):
        return pltpu.VMEM(shape, dtype)

    rows = (NX, 2, 64, lanes)
    sums = [vm(*rows), vm(NX // 2, 2, 64, lanes), vm(NX // 2, 2, 64, lanes), vm(64, lanes), vm(64, lanes)]
    return pl.pallas_call(
        attention_kernel,
        out_shape=(
            jax.ShapeDtypeStruct((2, 64, lanes), BF16),
            jax.ShapeDtypeStruct((2, 64, lanes), BF16),
            jax.ShapeDtypeStruct((2, chunk, 128), F32),
            jax.ShapeDtypeStruct(wq_own.shape, BF16),
            jax.ShapeDtypeStruct(wkv_own.shape, BF16),
        ),
        in_specs=[vmem, vmem, vmem, anywhere, anywhere],
        out_specs=(vmem, vmem, vmem, anywhere, anywhere),
        scratch_shapes=[
            vm(*rows), vm(*rows), vm(NZ, 2, chunk, 128), vm(NZ, 2, 128, chunk), vm(NX, 128, 4 * lanes),
            vm(tiles, chunk, lanes), vm(tiles + 7, lanes, dtype=F32), vm(NX, 3, 8, lanes, dtype=F32),
            vm(8, lanes, dtype=F32), vm(8, lanes, dtype=F32), vm(*rows, dtype=F32), vm(*rows, dtype=F32),
            vm(NZ, 2, chunk, 128, dtype=F32),
        ] + sums + sums + [
            vm(NZ, 2, chunk, 128), vm(NZ // 2, 2, chunk, 128), vm(NZ // 2, 2, chunk, 128),
            vm(chunk, 128), vm(chunk, 128),
            pltpu.SemaphoreType.DMA((copies,)),
            pltpu.SemaphoreType.DMA((copies,)),
            pltpu.SemaphoreType.DMA((5,)),
        ],
        compiler_params=pltpu.CompilerParams(
            collective_id=0, has_side_effects=True, vmem_limit_bytes=58 * 1024 * 1024
        ),
        name="attention",
    )(q_own, do_own, kv_own, wq_own, wkv_own)


def finish_kernel(
    g_own, proj, outp,
    g_all, proj_out, outp_out,
    proj_snd, proj_l, proj_r, proj_z, projz_snd, projz_l, projz_r,
    outp_snd, outp_l, outp_r, outp_x, outpx_snd, outpx_l, outpx_r,
    send_sems, recv_sems, copy_sem,
):
    x, z = seq_place()
    head = lax.axis_index("head")
    y, core = lax.div(head, 2), lax.rem(head, 2)
    right_x, left_x = seq_dev(mod(x + 1, NX), z), seq_dev(mod(x - 1, NX), z)
    right_z, left_z = seq_dev(x, mod(z + 1, NZ)), seq_dev(x, mod(z - 1, NZ))
    right_y, left_y = {"head": mod(y + 1, 4) * 2 + core}, {"head": mod(y - 1, 4) * 2 + core}
    twin = {"head": y * 2 + 1 - core}
    greet([right_x, left_x, right_z, left_z, right_y, left_y, twin])
    links = Links(send_sems, recv_sems)
    keep = pltpu.make_async_copy(g_own, g_all.at[head], copy_sem)
    keep.start()

    def slot(i, c):
        return g_all.at[i * 2 + c]

    def spread():
        rows = g_own.shape[0] // 2
        cut = (lambda ref: ref.at[0:rows], lambda ref: ref.at[rows : 2 * rows])
        ring = gather_ring(links, lambda i: slot(i, core), g_own, y, 4, right_y, left_y, cut)
        next(ring)
        got = [(links.send(g_own, slot(y, core), twin), y)]
        yield
        next(ring)
        for i in (mod(y - 1, 4), mod(y + 1, 4)):
            got.append((links.send(slot(i, core), slot(i, core), twin), i))
        yield
        for _ in ring:
            pass
        i = mod(y + 2, 4)
        got.append((links.send(slot(i, core), slot(i, core), twin), i))
        yield
        for index, i in got:
            links.arrived(index, slot(i, 1 - core))

    def halves(dim, size):
        low, high = slice(0, size // 2), slice(size // 2, size)
        if dim == 0:
            return (lambda ref: ref.at[low], lambda ref: ref.at[high])
        return (lambda ref: ref.at[:, low], lambda ref: ref.at[:, high])

    slab = proj.shape[2]

    def keep_to(ref):
        def write(value):
            ref[...] = value.astype(ref.dtype)

        return write

    def proj_sums():
        yield from scatter_ring(
            links, lambda i: proj.at[i], lambda i: proj_snd.at[i], lambda i: proj_l.at[i], lambda i: proj_r.at[i],
            x, NX, right_x, left_x, halves(0, NZ), keep_to(proj_z))
        yield from scatter_ring(
            links, lambda i: proj_z.at[i], lambda i: projz_snd.at[i], lambda i: projz_l.at[i], lambda i: projz_r.at[i],
            z, NZ, right_z, left_z, halves(0, slab), keep_to(proj_out))

    def outp_sums():
        yield from scatter_ring(
            links, lambda i: outp.at[:, i], lambda i: outp_snd.at[i], lambda i: outp_l.at[i], lambda i: outp_r.at[i],
            z, NZ, right_z, left_z, halves(0, NX), keep_to(outp_x))
        yield from scatter_ring(
            links, lambda i: outp_x.at[i], lambda i: outpx_snd.at[i], lambda i: outpx_l.at[i], lambda i: outpx_r.at[i],
            x, NX, right_x, left_x, halves(0, slab), keep_to(outp_out))

    together(proj_sums(), outp_sums(), spread())
    keep.wait()
    links.drain()


def finish(g_own, proj, outp):
    vmem = pl.BlockSpec(memory_space=pltpu.VMEM)
    _, _, slab, wide = proj.shape
    narrow = outp.shape[3]
    copies = 48

    def vm(*shape, dtype=BF16):
        return pltpu.VMEM(shape, dtype)

    return pl.pallas_call(
        finish_kernel,
        out_shape=(
            jax.ShapeDtypeStruct((NH,) + g_own.shape, BF16),
            jax.ShapeDtypeStruct((slab, wide), F32),
            jax.ShapeDtypeStruct((slab, narrow), F32),
        ),
        in_specs=[vmem] * 3,
        out_specs=(vmem,) * 3,
        scratch_shapes=[
            vm(NX, NZ, slab, wide), vm(NX // 2, NZ, slab, wide), vm(NX // 2, NZ, slab, wide),
            vm(NZ, slab, wide, dtype=F32), vm(NZ, slab, wide), vm(NZ // 2, slab, wide), vm(NZ // 2, slab, wide),
            vm(NZ, NX, slab, narrow), vm(NZ // 2, NX, slab, narrow), vm(NZ // 2, NX, slab, narrow),
            vm(NX, slab, narrow, dtype=F32), vm(NX, slab, narrow), vm(NX // 2, slab, narrow), vm(NX // 2, slab, narrow),
            pltpu.SemaphoreType.DMA((copies,)),
            pltpu.SemaphoreType.DMA((copies,)),
            pltpu.SemaphoreType.DMA,
        ],
        compiler_params=pltpu.CompilerParams(
            collective_id=1, has_side_effects=True, vmem_limit_bytes=40 * 1024 * 1024
        ),
        name="finish",
    )(g_own, proj, outp)


def body(inputs, out_grad, w_query, w_key, w_value, w_output):
    tokens = inputs.shape[0]
    chunk = tokens // 2
    model = inputs.shape[1]
    me = lax.axis_index("seq")
    positions = (me * tokens + jnp.arange(tokens, dtype=jnp.int32)).astype(F32)
    cos, sin = rotary(positions)
    cos_t, sin_t = cos.T, sin.T

    def halves(rows):
        return rows.reshape(2, HD, 2, chunk).transpose(2, 1, 0, 3).reshape(2, HD, 2 * chunk)

    q = jnp.einsum("td,df->ft", inputs, w_query, preferred_element_type=F32).reshape(2, HD, tokens)
    front, back = q[:, :32], q[:, 32:]
    q = jnp.concatenate([front * cos_t - back * sin_t, back * cos_t + front * sin_t], 1).astype(BF16)
    q = q * jnp.asarray(0.125, BF16)
    do = jnp.einsum("td,fd->ft", out_grad, w_output, preferred_element_type=F32).astype(BF16)
    w_kv = jnp.concatenate([w_key, w_value], 1)
    kv = jnp.dot(inputs, w_kv, preferred_element_type=F32)
    front, back = kv[:, :32], kv[:, 32:64]
    kv = jnp.concatenate([front * cos - back * sin, back * cos + front * sin, kv[:, 64:]], 1)
    kv = kv.astype(BF16).reshape(2, chunk, 128)

    o, dq, dkv, wq_all, wkv_all = attention(
        halves(q), halves(do), kv, w_query.reshape(NH, model // NH, 128), w_kv.reshape(NH, model // NH, 128)
    )

    def whole(rows):
        return rows.reshape(2, HD, 2, chunk).transpose(2, 1, 0, 3).reshape(2, HD, tokens)

    o = whole(o).reshape(128, tokens)
    dq = whole(dq).astype(F32)
    front, back = dq[:, :32], dq[:, 32:]
    dq = jnp.concatenate([front * cos_t + back * sin_t, back * cos_t - front * sin_t], 1)
    dq = dq.astype(BF16).reshape(128, tokens).T
    dkv = dkv.reshape(tokens, 128)
    front, back = dkv[:, :32], dkv[:, 32:64]
    g = jnp.concatenate(
        [
            dq,
            (front * cos + back * sin).astype(BF16),
            (back * cos - front * sin).astype(BF16),
            dkv[:, 64:].astype(BF16),
        ],
        1,
    )
    slab = model // (NX * NZ)
    proj = jnp.einsum("tc,tf->cf", inputs, g, preferred_element_type=F32).astype(BF16)
    outp = jnp.einsum("tc,ft->cf", out_grad, o, preferred_element_type=F32).astype(BF16)
    g_all, proj_sum, outp_sum = finish(
        g, proj.reshape(NX, NZ, slab, 256), outp.reshape(NX, NZ, slab, 128)
    )
    grad_inputs = jnp.einsum("htf,hcf->tc", g_all[..., :128], wq_all, preferred_element_type=F32)
    grad_inputs += jnp.einsum("htf,hcf->tc", g_all[..., 128:], wkv_all, preferred_element_type=F32)
    grad_inputs = grad_inputs.astype(BF16)
    return grad_inputs, proj_sum[:, :128], proj_sum[:, 128:192], proj_sum[:, 192:], outp_sum.T


def solution(mesh):
    placed = (
        P("seq", None),
        P("seq", None),
        P(None, "head"),
        P(None, "head"),
        P(None, "head"),
        P("head", None),
    )
    return jax.shard_map(
        body,
        mesh=mesh,
        in_specs=placed,
        out_specs=(
            P("seq", "head"),
            P("seq", "head"),
            P("seq", "head"),
            P("seq", "head"),
            P("head", "seq"),
        ),
        check_vma=False,
    )
```

```python
import functools

import jax
import jax.numpy as jnp
from jax import lax
from jax.experimental import pallas as pl
from jax.experimental.pallas import tpu as pltpu
from jax.sharding import PartitionSpec as P

HD = 64
NX, NZ, NH = 4, 8, 8
ROPE_BASE = 500000.0
NEG = -1e30
F32, BF16 = jnp.float32, jnp.bfloat16
MESH = pl.DeviceIdType.MESH


def rotary(positions):
    half_dim = HD // 2
    frequency = ROPE_BASE ** (-(jnp.arange(half_dim, dtype=jnp.float32) * 2.0 / HD))
    angles = positions[:, None] * frequency[None, :]
    return jnp.cos(angles), jnp.sin(angles)


def mod(value, size):
    return lax.rem(value + 2 * size, size)


class Links:
    def __init__(self, send_sems, recv_sems):
        self.send_sems, self.recv_sems = send_sems, recv_sems
        self.used, self.open = 0, []

    def send(self, src, dst, device):
        index = self.used
        self.used += 1
        copy = pltpu.make_async_remote_copy(
            src_ref=src,
            dst_ref=dst,
            send_sem=self.send_sems.at[index],
            recv_sem=self.recv_sems.at[index],
            device_id=device,
            device_id_type=MESH,
        )
        copy.start()
        self.open.append(copy)
        return index

    def arrived(self, index, landing):
        pltpu.make_async_copy(landing, landing, self.recv_sems.at[index]).wait()

    def drain(self):
        for copy in self.open:
            copy.wait_send()
        self.open = []


def together(*streams):
    streams = list(streams)
    while streams:
        for stream in list(streams):
            try:
                next(stream)
            except StopIteration:
                streams.remove(stream)


def gather_ring(links, slots, own, where, size, right, left, cut):
    far = size // 2
    low, high = cut
    held_r, held_l = own, own
    for step in range(1, far + 1):
        slot_r, slot_l = mod(where - step + 1, size), mod(where + step - 1, size)
        if step == far:
            held_r, held_l = low(held_r), high(held_l)
            place_r, place_l = low(slots(slot_r)), high(slots(slot_l))
        else:
            place_r, place_l = slots(slot_r), slots(slot_l)
        got_r = links.send(held_r, place_r, right)
        got_l = links.send(held_l, place_l, left)
        yield
        held_r, held_l = slots(mod(where - step, size)), slots(mod(where + step, size))
        if step == far:
            links.arrived(got_r, low(held_r))
            links.arrived(got_l, high(held_l))
        else:
            links.arrived(got_r, held_r)
            links.arrived(got_l, held_l)


def scatter_ring(links, mine, snd, from_left, from_right, where, size, right, left, cut, finish):
    far = size // 2
    low, high = cut
    owner = mod(where + far, size)
    snd(owner)[...] = mine(owner)[...].astype(BF16)
    got_r = links.send(low(snd(owner)), low(from_left(0)), right)
    got_l = links.send(high(snd(owner)), high(from_right(0)), left)
    for step in range(2, far + 1):
        yield
        for got, came, place, sign, part, target in (
            (got_r, from_left, from_left, 1, low, right),
            (got_l, from_right, from_right, -1, high, left),
        ):
            owner = mod(where + sign * (far - step + 1), size)
            if step == 2:
                links.arrived(got, part(came(0)))
                other = high if part is low else low
                part(snd(owner))[...] = (
                    part(mine(owner))[...].astype(F32) + part(came(0))[...].astype(F32)
                ).astype(BF16)
                other(snd(owner))[...] = other(mine(owner))[...].astype(BF16)
            else:
                links.arrived(got, came(step - 2))
                snd(owner)[...] = (
                    mine(owner)[...].astype(F32) + came(step - 2)[...].astype(F32)
                ).astype(BF16)
            sent = links.send(snd(owner), place(step - 1), target)
            if sign == 1:
                got_r = sent
            else:
                got_l = sent
    yield
    links.arrived(got_r, from_left(far - 1))
    links.arrived(got_l, from_right(far - 1))
    finish(
        mine(where)[...].astype(F32)
        + from_left(far - 1)[...].astype(F32)
        + from_right(far - 1)[...].astype(F32)
    )


def seq_place():
    me = lax.axis_index("seq")
    return lax.div(me, NZ), lax.rem(me, NZ)


def seq_dev(x, z):
    return {"seq": x * NZ + z}


def nn(a, b):
    return lax.dot_general(a, b, (((1,), (0,)), ((), ())), preferred_element_type=F32)


def nt(a, b):
    return lax.dot_general(a, b, (((1,), (1,)), ((), ())), preferred_element_type=F32)


def fold(values, op):
    return op(values.reshape(values.shape[0] // 8, 8, values.shape[1]), axis=0)


def layer_kernel(
    inputs, out_grad, w_query, w_key, w_value, w_output, cos_t, sin_t,
    gi_out, gq_out, gk_out, gv_out, go_out,
    x_v, g_v, w_cat, wk_v, wv_v, wo_v, w_all, x_t,
    q_own, do_own, kv_own,
    qg, dg, kv, kvt, both, probs, tops, stats, lse, delta, o_sum, dq_sum, dkv,
    ring_o, o_in, ring_q, q_in, o_t, g_t,
    dkv_snd, dkv_l, dkv_r, dkv_back, dkv_land,
    proj_o, po_snd, po_l, po_r, po_x, po_xs, po_xi,
    proj_kv, pk_snd, pk_l, pk_r, pk_x, pk_xs, pk_xi,
    proj_q, pq_snd, pq_l, pq_r, pq_z, pq_zi,
    g_all, gi_sum,
    send_sems, recv_sems, copy_sems,
):
    x, z = seq_place()
    head = lax.axis_index("head")
    y, core = lax.div(head, 2), lax.rem(head, 2)
    chunk, lanes = kv_own.shape[1], q_own.shape[2]
    far_x, far_z = NX - 1 - x, NZ - 1 - z
    right_x, left_x = seq_dev(mod(x + 1, NX), z), seq_dev(mod(x - 1, NX), z)
    across_x, mirror_x = seq_dev(mod(x + 2, NX), z), seq_dev(far_x, z)
    right_z, left_z = seq_dev(x, mod(z + 1, NZ)), seq_dev(x, mod(z - 1, NZ))
    mirror_z = seq_dev(x, far_z)
    others = [{"head": mod(head + step, NH)} for step in range(1, NH)]
    right_y, left_y = {"head": mod(y + 1, 4) * 2 + core}, {"head": mod(y - 1, 4) * 2 + core}
    twin = {"head": y * 2 + 1 - core}

    loads = [
        pltpu.make_async_copy(source, target, copy_sems.at[n])
        for n, (source, target) in enumerate(
            (
                (w_query, w_cat.at[:, 0:128]),
                (w_key, wk_v),
                (w_value, wv_v),
                (inputs, x_v),
                (w_output, wo_v),
                (out_grad, g_v),
            )
        )
    ]
    for load in loads:
        load.start()
    partners = (
        [seq_dev(mod(x + step, NX), z) for step in range(1, NX)]
        + [seq_dev(x, mod(z + step, NZ)) for step in range(1, NZ)]
        + [seq_dev(mod(x + step, NX), far_z) for step in range(1, NX)]
        + others
    )
    barrier = pltpu.get_barrier_semaphore()
    for device in partners:
        pl.semaphore_signal(barrier, inc=1, device_id=device, device_id_type=MESH)
    links = Links(send_sems, recv_sems)

    for load in loads[:3]:
        load.wait()
    w_kv = jnp.concatenate([wk_v[...], wv_v[...]], 0)
    w_cat[:, 128:256] = w_kv.astype(F32).T.astype(BF16)
    loads[3].wait()

    def turn(rows, a, sign):
        cos, sin = (table[:, a * chunk : (a + 1) * chunk] for table in (cos_t, sin_t))
        front, back = rows[0:32], rows[32:64]
        return jnp.concatenate([front * cos - sign * back * sin, back * cos + sign * front * sin], 0)

    for a in range(2):
        rows = nn(x_v[a * chunk : (a + 1) * chunk, :], w_cat[...]).T
        q = jnp.concatenate([turn(rows[0:64], a, 1.0), turn(rows[64:128], a, 1.0)], 1).astype(BF16)
        q_own[a] = q * jnp.asarray(0.125, BF16)
        kv_own[a] = jnp.concatenate([turn(rows[128:192], a, 1.0), rows[192:256]], 0).T.astype(BF16)
    qg[x, 0] = q_own[0]
    kv[z, 0] = kv_own[0]
    pl.semaphore_wait(barrier, len(partners))

    sent_q = links.send(q_own.at[1], qg.at[x, 1], mirror_z)
    sent_kv = links.send(kv_own.at[1], kv.at[z, 1], mirror_x)
    rows_q = (lambda ref: ref.at[0:32], lambda ref: ref.at[32:64])
    rows_k = (lambda ref: ref.at[0 : chunk // 2], lambda ref: ref.at[chunk // 2 : chunk])

    def ring_x(ref, a, own):
        return gather_ring(links, lambda i: ref.at[i, a], own, x, NX, right_x, left_x, rows_q)

    def ring_z(a, own):
        return gather_ring(links, lambda i: kv.at[i, a], own, z, NZ, right_z, left_z, rows_k)

    def pump(*rings):
        for ring in rings:
            next(ring, None)

    q_a, k_a = ring_x(qg, 0, q_own.at[0]), ring_z(0, kv_own.at[0])
    q_b, k_b = ring_x(qg, 1, qg.at[x, 1]), ring_z(1, kv.at[z, 1])
    d_a, d_b = ring_x(dg, 0, do_own.at[0]), ring_x(dg, 1, dg.at[x, 1])
    pump(q_a, k_a)
    for load in loads[4:]:
        load.wait()
    for a in range(2):
        rows = nt(wo_v[...], g_v[a * chunk : (a + 1) * chunk, :]).astype(BF16)
        do_own[a] = jnp.concatenate([rows[0:64], rows[64:128]], 1)
    dg[x, 0] = do_own[0]
    links.arrived(sent_q, qg.at[x, 1])
    pump(q_b)
    links.arrived(sent_kv, kv.at[z, 1])
    pump(k_b)
    sent_do = links.send(do_own.at[1], dg.at[x, 1], mirror_z)
    dkv[...] = jnp.zeros(dkv.shape, F32)
    o_sum[...] = jnp.zeros(o_sum.shape, F32)
    dq_sum[...] = jnp.zeros(dq_sum.shape, F32)
    both[...] = jnp.zeros(both.shape, BF16)
    stats[x, 0] = jnp.full(stats.shape[2:], NEG, F32)
    stats[x, 1] = jnp.zeros(stats.shape[2:], F32)
    pump(q_a, k_a, q_b, k_b, d_a)
    links.arrived(sent_do, dg.at[x, 1])
    pump(d_b)

    def flip(n, _):
        part = pl.ds(pl.multiple_of(n * 128, 128), 128)
        x_t[part, :] = x_v[:, part].astype(F32).T.astype(BF16)
        return 0

    lax.fori_loop(0, x_t.shape[0] // 128, flip, 0)
    pump(q_a, q_b)

    def full_tiles(zc):
        tiles = []
        for n in range(3):
            first = n < far_x
            half, block = jnp.where(first, 0, 1), jnp.where(first, x + 1 + n, n + 1)
            tiles += [(half, block, a, zc * 6 + n * 2 + a) for a in range(2)]
        return tiles

    def cross_tiles(zc, a):
        base = 6 * NZ + (0 if a == 0 else 2 * z + 1) + 2 * zc
        return [(0, x, a, base), (1, far_x, a, base + 1)]

    def forward(zc, tiles, cut=()):
        found = []
        for n, (half, block, a, place) in enumerate(tiles):
            s = nn(kv[zc, half][:, 0:64], qg[block, a])
            if n in cut:
                key = lax.broadcasted_iota(jnp.int32, (chunk, lanes), 0)
                row = lax.rem(lax.broadcasted_iota(jnp.int32, (chunk, lanes), 1), chunk)
                on_diagonal = zc == (z if a == 0 else far_z)
                s = jnp.where(row - key >= jnp.where(on_diagonal, 0, -chunk), s, NEG)
            found.append(s)
        highs = [jnp.max(fold(s, jnp.max), axis=0, keepdims=True) for s in found]
        raised = [jnp.exp(s - high) for s, high in zip(found, highs)]
        lows = [p.astype(BF16) for p in raised]
        totals = [jnp.sum(fold(p, jnp.sum), axis=0, keepdims=True) for p in raised]
        for (_, _, _, place), low, high in zip(tiles, lows, highs):
            probs[place] = low
            tops[pl.ds(place, 1), :] = high
        outs = [nn(kvt[zc, half, 64:128, :], low) for (half, _, _, _), low in zip(tiles, lows)]
        for (_, block, a, _), high, total, out in zip(tiles, highs, totals, outs):
            group = pl.ds(block * 2 + a, 1)
            old = stats[x, 0, group, :]
            top = jnp.maximum(old, high)
            keep, add = jnp.exp(old - top), jnp.exp(high - top)
            stats[x, 0, group, :] = top
            stats[x, 1, group, :] = stats[x, 1, group, :] * keep + total * add
            o_sum[block, a] = o_sum[block, a] * keep + out * add

    def forward_slot(zc):
        for half in range(2):
            kvt[zc, half] = kv[zc, half].astype(F32).T.astype(BF16)
        forward(zc, full_tiles(zc))
        pl.when(zc < z)(lambda: forward(zc, cross_tiles(zc, 0)))
        pl.when(zc == z)(lambda: forward(zc, cross_tiles(zc, 0)[:1], (0,)))
        pl.when(zc <= far_z)(lambda: forward(zc, cross_tiles(zc, 1), (1,)))

    def slots(work, distances):
        def one(n, _):
            work(mod(z + distances[0] + n * (distances[-1] - distances[0]), NZ))
            return 0

        lax.fori_loop(0, len(distances), one, 0)

    slots(forward_slot, (0,))
    pump(k_a, k_b, d_a, d_b)
    slots(forward_slot, (1, -1))
    pump(k_a, k_b, d_a, d_b)
    slots(forward_slot, (2, -2))
    pump(k_a, k_b)
    slots(forward_slot, (3, -3))
    slots(forward_slot, (4,))

    weights = []
    for step in range(1, NH):
        rows = pl.ds(pl.multiple_of(mod(head + step, NH) * w_all.shape[1], w_all.shape[1]), w_all.shape[1])
        weights.append((links.send(w_cat.at[rows], w_all.at[head], others[step - 1]), step))
    rows = pl.ds(pl.multiple_of(head * w_all.shape[1], w_all.shape[1]), w_all.shape[1])
    w_all[head] = w_cat[rows, :]

    for block in range(NX):
        for a in range(2):
            group = block * 2 + a
            stats[x, 2, group : group + 1, :] = jnp.sum(
                o_sum[block, a] * dg[block, a].astype(F32), axis=0, keepdims=True
            )
    shares = [
        (links.send(stats.at[x], stats.at[x], device), mod(x - step, NX))
        for step, device in ((1, right_x), (2, across_x), (3, left_x))
    ]
    for block in range(NX):
        for a in range(2):
            both[block, 0:64, a * lanes : (a + 1) * lanes] = qg[block, a]
            both[block, 64:128, (2 + a) * lanes : (3 + a) * lanes] = dg[block, a]
    for index, source in shares:
        links.arrived(index, stats.at[source])
    top = functools.reduce(jnp.maximum, [stats[n, 0] for n in range(NX)])
    part = [jnp.exp(stats[n, 0] - top) for n in range(NX)]
    total = sum(stats[n, 1] * part[n] for n in range(NX))
    lse[...] = top + jnp.log(total)
    delta[...] = sum(stats[n, 2] * part[n] for n in range(NX)) / total
    share = jnp.exp(stats[x, 0] - lse[...])
    for block in range(NX):
        for a in range(2):
            group = block * 2 + a
            ring_o[block, a] = (o_sum[block, a] * share[group : group + 1]).astype(BF16)

    def backward_tile(zc, half, block, a, place):
        group = pl.ds(block * 2 + a, 1)
        scale = jnp.exp(tops[pl.ds(place, 1), :] - lse[group, :])
        p = probs[place] * scale.astype(BF16)
        dp = nn(kv[zc, half], both[block, :, (2 + a) * lanes : (3 + a) * lanes])
        return p, p * (dp - delta[group, :]).astype(BF16)

    def backward_full(zc):
        tiles = full_tiles(zc)
        done = [backward_tile(zc, *tile) for tile in tiles]
        for (half, block, a, _), (_, ds) in zip(tiles, done):
            dq_sum[block, a] += nn(kvt[zc, half, 0:64, :], ds)
        for n in range(3):
            half, block = tiles[2 * n][:2]
            (p0, ds0), (p1, ds1) = done[2 * n], done[2 * n + 1]
            dkv[zc, half] += nt(jnp.concatenate([ds0, ds1, p0, p1], 1), both[block])

    def backward_some(zc, tiles):
        done = [backward_tile(zc, *tile) for tile in tiles]
        for (half, block, a, _), (p, ds) in zip(tiles, done):
            dq_sum[block, a] += nn(kvt[zc, half, 0:64, :], ds)
            dkv[zc, half] += nt(ds, both[block, :, a * lanes : (a + 1) * lanes]) + nt(
                p, both[block, :, (2 + a) * lanes : (3 + a) * lanes]
            )

    def backward_slot(zc):
        backward_full(zc)
        pl.when(zc < z)(lambda: backward_some(zc, cross_tiles(zc, 0)))
        pl.when(zc == z)(lambda: backward_some(zc, cross_tiles(zc, 0)[:1]))
        pl.when(zc <= far_z)(lambda: backward_some(zc, cross_tiles(zc, 1)))

    pair_k = (lambda ref: ref.at[:, 0 : chunk // 2], lambda ref: ref.at[:, chunk // 2 : chunk])

    def send_home(parts, into):
        got = []
        for step in range(1, NX):
            there = mod(x + step, NX)
            got.append((links.send(parts.at[there, 0], into.at[x, 0], seq_dev(there, z)), mod(x - step, NX), 0))
        for step in range(NX):
            there = mod(x + step, NX)
            got.append((links.send(parts.at[there, 1], into.at[x, 1], seq_dev(there, far_z)), mod(x - step, NX), 1))
        return got

    def collect(parts, into, got):
        total = [parts[x, 0].astype(F32), 0.0]
        for index, source, a in got:
            links.arrived(index, into.at[source, a])
            total[a] = total[a] + into[source, a].astype(F32)
        return total

    def keep_in(ref):
        def write(value):
            ref[...] = value.astype(ref.dtype)

        return write

    def sums_zx(proj, snd, from_l, from_r, mid, mid_snd, mid_in, write):
        yield from scatter_ring(links, lambda i: proj.at[:, i], lambda i: snd.at[i], lambda i: from_l.at[i],
                                lambda i: from_r.at[i], z, NZ, right_z, left_z,
                                (lambda ref: ref.at[0 : NX // 2], lambda ref: ref.at[NX // 2 : NX]),
                                keep_in(mid))
        mid_snd[...] = mid[...].astype(BF16)
        got = [
            links.send(mid_snd.at[mod(x + step, NX)], mid_in.at[x], seq_dev(mod(x + step, NX), z))
            for step in range(1, NX)
        ]
        yield
        total = mid[x]
        for step in range(1, NX):
            links.arrived(got[step - 1], mid_in.at[mod(x - step, NX)])
            total = total + mid_in[mod(x - step, NX)].astype(F32)
        write(total)

    def sums_xz(proj, snd, from_l, from_r, mid, mid_in, write):
        yield from scatter_ring(links, lambda i: proj.at[i], lambda i: snd.at[i], lambda i: from_l.at[i],
                                lambda i: from_r.at[i], x, NX, right_x, left_x,
                                (lambda ref: ref.at[0 : NZ // 2], lambda ref: ref.at[NZ // 2 : NZ]),
                                keep_in(mid))
        got = [
            links.send(mid.at[mod(z + step, NZ)], mid_in.at[z], seq_dev(x, mod(z + step, NZ)))
            for step in range(1, NZ)
        ]
        yield
        total = mid[z].astype(F32)
        for step in range(1, NZ):
            links.arrived(got[step - 1], mid_in.at[mod(z - step, NZ)])
            total = total + mid_in[mod(z - step, NZ)].astype(F32)
        write(total)

    def spread(part):
        rows = g_t.shape[1] // 2
        cut = (lambda ref: ref.at[0:rows], lambda ref: ref.at[rows : 2 * rows])

        def slot(i, c):
            return g_all.at[i * 2 + c, part]

        own = g_t.at[part]
        ring = gather_ring(links, lambda i: slot(i, core), own, y, 4, right_y, left_y, cut)
        next(ring)
        got = [(links.send(own, slot(y, core), twin), y)]
        g_all[head, part] = g_t[part]
        yield
        next(ring)
        for i in (mod(y - 1, 4), mod(y + 1, 4)):
            got.append((links.send(slot(i, core), slot(i, core), twin), i))
        yield
        for _ in ring:
            pass
        i = mod(y + 2, 4)
        got.append((links.send(slot(i, core), slot(i, core), twin), i))
        yield
        for index, i in got:
            links.arrived(index, slot(i, 1 - core))

    def project(proj, rows):
        def one(i, _):
            part = pl.ds(pl.multiple_of(i * 512, 512), 512)
            proj[i] = nt(x_t[part, :], rows[...]).astype(BF16).reshape(proj.shape[1:])
            return 0

        lax.fori_loop(0, NX, one, 0)

    def write_kv(value):
        gk_out[...] = value[:, 0:64]
        gv_out[...] = value[:, 64:128]

    kv_home = []

    def finish_kv(value):
        kv_home.append(value[0])
        dkv_back[...] = value[1].astype(BF16)
        kv_home.append(links.send(dkv_back, dkv_land, mirror_x))

    kv_ring = scatter_ring(links, lambda i: dkv.at[i], lambda i: dkv_snd.at[i], lambda i: dkv_l.at[i],
                           lambda i: dkv_r.at[i], z, NZ, right_z, left_z, pair_k, finish_kv)
    o_proj = sums_zx(proj_o, po_snd, po_l, po_r, po_x, po_xs, po_xi, keep_in(go_out))
    got_o = send_home(ring_o, o_in)
    slots(backward_slot, (4,))
    pump(kv_ring)
    slots(backward_slot, (3, -3))
    pump(kv_ring)
    for a, rows in enumerate(collect(ring_o, o_in, got_o)):
        for h in range(2):
            o_t[h * 64 : (h + 1) * 64, a * chunk : (a + 1) * chunk] = rows[
                :, h * chunk : (h + 1) * chunk
            ].astype(BF16)

    def project_o(i, _):
        part = pl.ds(pl.multiple_of(i * 512, 512), 512)
        proj_o[i] = nn(o_t[...], g_v[:, part]).T.astype(BF16).reshape(proj_o.shape[1:])
        return 0

    lax.fori_loop(0, NX, project_o, 0)
    pump(o_proj)
    slots(backward_slot, (2, -2))
    pump(kv_ring, o_proj)
    slots(backward_slot, (1, -1))
    pump(kv_ring, o_proj)
    slots(backward_slot, (0,))
    for block in range(NX):
        for a in range(2):
            ring_q[block, a] = (dq_sum[block, a] * 0.125).astype(BF16)
    got_q = send_home(ring_q, q_in)
    pump(kv_ring, o_proj)

    def place_kv(a, rows):
        columns = slice(a * chunk, (a + 1) * chunk)
        g_t[1, 0:64, columns] = turn(rows[0:64], a, -1.0).astype(BF16)
        g_t[1, 64:128, columns] = rows[64:128].astype(BF16)

    place_kv(0, kv_home[0].T)
    pump(o_proj)
    links.arrived(kv_home[1], dkv_land)
    place_kv(1, dkv_land[...].astype(F32).T)
    gather_kv = spread(1)
    pump(gather_kv)
    project(proj_kv, g_t.at[1])
    kv_proj = sums_zx(proj_kv, pk_snd, pk_l, pk_r, pk_x, pk_xs, pk_xi, write_kv)
    pump(kv_proj, o_proj)
    for a, rows in enumerate(collect(ring_q, q_in, got_q)):
        for h in range(2):
            g_t[0, h * 64 : (h + 1) * 64, a * chunk : (a + 1) * chunk] = turn(
                rows[:, h * chunk : (h + 1) * chunk], a, -1.0
            ).astype(BF16)
    gather_q = spread(0)
    pump(gather_q, gather_kv, kv_proj)
    project(proj_q, g_t.at[0])
    q_proj = sums_xz(proj_q, pq_snd, pq_l, pq_r, pq_z, pq_zi, keep_in(gq_out))
    pump(q_proj, kv_proj, gather_kv, q_proj, gather_q, kv_proj, gather_kv, q_proj, kv_proj)

    for index, step in weights:
        links.arrived(index, w_all.at[mod(head - step, NH)])
    gi_sum[...] = sum(nn(w_all[n, :, 128:256], g_all[n, 1]) for n in range(NH))
    together(gather_q, kv_proj, q_proj, o_proj, gather_kv)
    total = gi_sum[...] + sum(nn(w_all[n, :, 0:128], g_all[n, 0]) for n in range(NH))
    gi_out[...] = total.T.astype(BF16)
    links.drain()


def layer(inputs, out_grad, w_query, w_key, w_value, w_output, cos_t, sin_t):
    tokens, model = inputs.shape
    chunk, lanes = tokens // 2, tokens
    slab = model // (NX * NZ)
    tiles = (2 * NX * 2 * NZ) // 2 + 1
    vmem = pl.BlockSpec(memory_space=pltpu.VMEM)
    anywhere = pl.BlockSpec(memory_space=pl.ANY)
    copies = 120

    def vm(*shape, dtype=BF16):
        return pltpu.VMEM(shape, dtype)

    rows = (NX, 2, 64, lanes)

    def sums_zx():
        return [
            vm(NX, NZ, slab, 128), vm(NZ, NX, slab, 128), vm(NZ // 2, NX, slab, 128), vm(NZ // 2, NX, slab, 128),
            vm(NX, slab, 128, dtype=F32), vm(NX, slab, 128), vm(NX, slab, 128),
        ]

    return pl.pallas_call(
        layer_kernel,
        out_shape=(
            jax.ShapeDtypeStruct((tokens, 256), BF16),
            jax.ShapeDtypeStruct((slab, 128), F32),
            jax.ShapeDtypeStruct((slab, 64), F32),
            jax.ShapeDtypeStruct((slab, 64), F32),
            jax.ShapeDtypeStruct((slab, 128), F32),
        ),
        in_specs=[anywhere] * 6 + [vmem] * 2,
        out_specs=(vmem,) * 5,
        scratch_shapes=[
            vm(tokens, model), vm(tokens, model), vm(model, 256), vm(64, model), vm(64, model), vm(128, model),
            vm(NH, model // NH, 256), vm(model, tokens),
            vm(2, 64, lanes), vm(2, 64, lanes), vm(2, chunk, 128),
            vm(*rows), vm(*rows), vm(NZ, 2, chunk, 128), vm(NZ, 2, 128, chunk), vm(NX, 128, 4 * lanes),
            vm(tiles, chunk, lanes), vm(tiles + 7, lanes, dtype=F32), vm(NX, 3, 8, lanes, dtype=F32),
            vm(8, lanes, dtype=F32), vm(8, lanes, dtype=F32), vm(*rows, dtype=F32), vm(*rows, dtype=F32),
            vm(NZ, 2, chunk, 128, dtype=F32),
            vm(*rows), vm(*rows), vm(*rows), vm(*rows), vm(128, tokens), vm(2, 128, tokens),
            vm(NZ, 2, chunk, 128), vm(NZ // 2, 2, chunk, 128), vm(NZ // 2, 2, chunk, 128),
            vm(chunk, 128), vm(chunk, 128),
        ] + sums_zx() + sums_zx() + [
            vm(NX, NZ, slab, 128), vm(NX, NZ, slab, 128), vm(NX // 2, NZ, slab, 128), vm(NX // 2, NZ, slab, 128),
            vm(NZ, slab, 128), vm(NZ, slab, 128),
            vm(NH, 2, 128, tokens), vm(256, tokens, dtype=F32),
            pltpu.SemaphoreType.DMA((copies,)),
            pltpu.SemaphoreType.DMA((copies,)),
            pltpu.SemaphoreType.DMA((6,)),
        ],
        compiler_params=pltpu.CompilerParams(
            collective_id=0, has_side_effects=True, vmem_limit_bytes=60 * 1024 * 1024
        ),
        name="layer",
    )(inputs, out_grad, w_query, w_key, w_value, w_output, cos_t, sin_t)


def hand_on_kernel(*refs):
    count = len(refs) // 2
    for source, target in zip(refs[:count], refs[count:]):
        target[...] = source[...]


def hand_on(arrays):
    vmem = pl.BlockSpec(memory_space=pltpu.VMEM)
    return pl.pallas_call(
        hand_on_kernel,
        out_shape=tuple(jax.ShapeDtypeStruct(array.shape, array.dtype) for array in arrays),
        in_specs=[vmem] * len(arrays),
        out_specs=(vmem,) * len(arrays),
        name="hand_on",
    )(*arrays)


def body(inputs, out_grad, w_query, w_key, w_value, w_output):
    tokens = inputs.shape[0]
    me = lax.axis_index("seq")
    positions = (me * tokens + jnp.arange(tokens, dtype=jnp.int32)).astype(F32)
    cos, sin = rotary(positions)
    results = layer(inputs, out_grad, w_query, w_key.T, w_value.T, w_output, cos.T, sin.T)
    *grads, grad_output = hand_on(results)
    return (*grads, grad_output.T)


def solution(mesh):
    placed = (
        P("seq", None),
        P("seq", None),
        P(None, "head"),
        P(None, "head"),
        P(None, "head"),
        P("head", None),
    )
    return jax.shard_map(
        body,
        mesh=mesh,
        in_specs=placed,
        out_specs=(
            P("seq", "head"),
            P("seq", "head"),
            P("seq", "head"),
            P("seq", "head"),
            P("head", "seq"),
        ),
        check_vma=False,
    )
```

```python
import functools

import jax
import jax.numpy as jnp
from jax import lax
from jax.experimental import pallas as pl
from jax.experimental.pallas import tpu as pltpu
from jax.sharding import PartitionSpec as P

HD = 64
NX, NZ, NH = 4, 8, 8
ROPE_BASE = 500000.0
NEG = -1e30
F32, BF16 = jnp.float32, jnp.bfloat16
MESH = pl.DeviceIdType.MESH


def rotary(positions):
    half_dim = HD // 2
    frequency = ROPE_BASE ** (-(jnp.arange(half_dim, dtype=jnp.float32) * 2.0 / HD))
    angles = positions[:, None] * frequency[None, :]
    return jnp.cos(angles), jnp.sin(angles)


def mod(value, size):
    return lax.rem(value + 2 * size, size)


class Links:
    def __init__(self, send_sems, recv_sems):
        self.send_sems, self.recv_sems = send_sems, recv_sems
        self.used, self.open = 0, []

    def send(self, src, dst, device):
        index = self.used
        self.used += 1
        copy = pltpu.make_async_remote_copy(
            src_ref=src,
            dst_ref=dst,
            send_sem=self.send_sems.at[index],
            recv_sem=self.recv_sems.at[index],
            device_id=device,
            device_id_type=MESH,
        )
        copy.start()
        self.open.append(copy)
        return index

    def arrived(self, index, landing):
        pltpu.make_async_copy(landing, landing, self.recv_sems.at[index]).wait()

    def drain(self):
        for copy in self.open:
            copy.wait_send()
        self.open = []


def together(*streams):
    streams = list(streams)
    while streams:
        for stream in list(streams):
            try:
                next(stream)
            except StopIteration:
                streams.remove(stream)


def gather_ring(links, slots, own, where, size, right, left, cut):
    far = size // 2
    low, high = cut
    held_r, held_l = own, own
    for step in range(1, far + 1):
        slot_r, slot_l = mod(where - step + 1, size), mod(where + step - 1, size)
        if step == far:
            held_r, held_l = low(held_r), high(held_l)
            place_r, place_l = low(slots(slot_r)), high(slots(slot_l))
        else:
            place_r, place_l = slots(slot_r), slots(slot_l)
        got_r = links.send(held_r, place_r, right)
        got_l = links.send(held_l, place_l, left)
        yield
        held_r, held_l = slots(mod(where - step, size)), slots(mod(where + step, size))
        if step == far:
            links.arrived(got_r, low(held_r))
            links.arrived(got_l, high(held_l))
        else:
            links.arrived(got_r, held_r)
            links.arrived(got_l, held_l)


def scatter_ring(links, mine, snd, from_left, from_right, where, size, right, left, cut, finish):
    far = size // 2
    low, high = cut
    owner = mod(where + far, size)
    snd(owner)[...] = mine(owner)[...].astype(BF16)
    got_r = links.send(low(snd(owner)), low(from_left(0)), right)
    got_l = links.send(high(snd(owner)), high(from_right(0)), left)
    for step in range(2, far + 1):
        yield
        for got, came, place, sign, part, target in (
            (got_r, from_left, from_left, 1, low, right),
            (got_l, from_right, from_right, -1, high, left),
        ):
            owner = mod(where + sign * (far - step + 1), size)
            if step == 2:
                links.arrived(got, part(came(0)))
                other = high if part is low else low
                part(snd(owner))[...] = (
                    part(mine(owner))[...].astype(F32) + part(came(0))[...].astype(F32)
                ).astype(BF16)
                other(snd(owner))[...] = other(mine(owner))[...].astype(BF16)
            else:
                links.arrived(got, came(step - 2))
                snd(owner)[...] = (
                    mine(owner)[...].astype(F32) + came(step - 2)[...].astype(F32)
                ).astype(BF16)
            sent = links.send(snd(owner), place(step - 1), target)
            if sign == 1:
                got_r = sent
            else:
                got_l = sent
    yield
    links.arrived(got_r, from_left(far - 1))
    links.arrived(got_l, from_right(far - 1))
    finish(
        mine(where)[...].astype(F32)
        + from_left(far - 1)[...].astype(F32)
        + from_right(far - 1)[...].astype(F32)
    )


def seq_place():
    me = lax.axis_index("seq")
    return lax.div(me, NZ), lax.rem(me, NZ)


def seq_dev(x, z):
    return {"seq": x * NZ + z}


def nn(a, b):
    return lax.dot_general(a, b, (((1,), (0,)), ((), ())), preferred_element_type=F32)


def nt(a, b):
    return lax.dot_general(a, b, (((1,), (1,)), ((), ())), preferred_element_type=F32)


def fold(values, op):
    return op(values.reshape(values.shape[0] // 8, 8, values.shape[1]), axis=0)


def layer_kernel(
    inputs, out_grad, w_query, w_key, w_value, w_output, cos_t, sin_t,
    gi_out, gq_out, gk_out, gv_out, go_out,
    x_v, g_v, w_cat, wk_v, wv_v, wo_v, w_all, x_t,
    q_own, do_own, kv_own,
    qg, dg, kv, kvt, both, probs, tops, stats, lse, delta, o_sum, dq_sum, dkv,
    ring_o, o_in, o_back, o_land, ring_q, q_in, q_back, q_land, o_t, g_t,
    dkv_snd, dkv_l, dkv_r, dkv_back, dkv_land,
    proj_o, po_in, po_mid, po_mid_in,
    proj_kv, pk_in, pk_mid, pk_mid_in,
    proj_q, pq_in, pq_mid, pq_mid_in,
    g_all, gi_sum,
    send_sems, recv_sems, copy_sems,
):
    x, z = seq_place()
    head = lax.axis_index("head")
    y, core = lax.div(head, 2), lax.rem(head, 2)
    chunk, lanes = kv_own.shape[1], q_own.shape[2]
    far_x, far_z = NX - 1 - x, NZ - 1 - z
    right_x, left_x = seq_dev(mod(x + 1, NX), z), seq_dev(mod(x - 1, NX), z)
    across_x, mirror_x = seq_dev(mod(x + 2, NX), z), seq_dev(far_x, z)
    right_z, left_z = seq_dev(x, mod(z + 1, NZ)), seq_dev(x, mod(z - 1, NZ))
    mirror_z = seq_dev(x, far_z)
    others = [{"head": mod(head + step, NH)} for step in range(1, NH)]
    right_y, left_y = {"head": mod(y + 1, 4) * 2 + core}, {"head": mod(y - 1, 4) * 2 + core}
    twin = {"head": y * 2 + 1 - core}

    loads = [
        pltpu.make_async_copy(source, target, copy_sems.at[n])
        for n, (source, target) in enumerate(
            (
                (w_query, w_cat.at[:, 0:128]),
                (w_key, wk_v),
                (w_value, wv_v),
                (inputs, x_v),
                (w_output, wo_v),
                (out_grad, g_v),
            )
        )
    ]
    for load in loads:
        load.start()
    partners = (
        [seq_dev(mod(x + step, NX), z) for step in range(1, NX)]
        + [seq_dev(x, mod(z + step, NZ)) for step in range(1, NZ)]
        + others
    )
    barrier = pltpu.get_barrier_semaphore()
    for device in partners:
        pl.semaphore_signal(barrier, inc=1, device_id=device, device_id_type=MESH)
    links = Links(send_sems, recv_sems)

    for load in loads[:3]:
        load.wait()
    w_kv = jnp.concatenate([wk_v[...], wv_v[...]], 0)
    w_cat[:, 128:256] = w_kv.astype(F32).T.astype(BF16)
    loads[3].wait()

    def turn(rows, a, sign):
        cos, sin = (table[:, a * chunk : (a + 1) * chunk] for table in (cos_t, sin_t))
        front, back = rows[0:32], rows[32:64]
        return jnp.concatenate([front * cos - sign * back * sin, back * cos + sign * front * sin], 0)

    for a in range(2):
        rows = nn(x_v[a * chunk : (a + 1) * chunk, :], w_cat[...]).T
        q = jnp.concatenate([turn(rows[0:64], a, 1.0), turn(rows[64:128], a, 1.0)], 1).astype(BF16)
        q_own[a] = q * jnp.asarray(0.125, BF16)
        kv_own[a] = jnp.concatenate([turn(rows[128:192], a, 1.0), rows[192:256]], 0).T.astype(BF16)
    qg[x, 0] = q_own[0]
    kv[z, 0] = kv_own[0]
    pl.semaphore_wait(barrier, len(partners))

    sent_q = links.send(q_own.at[1], qg.at[x, 1], mirror_z)
    sent_kv = links.send(kv_own.at[1], kv.at[z, 1], mirror_x)
    rows_q = (lambda ref: ref.at[0:32], lambda ref: ref.at[32:64])
    rows_k = (lambda ref: ref.at[0 : chunk // 2], lambda ref: ref.at[chunk // 2 : chunk])

    def ring_x(ref, a, own):
        return gather_ring(links, lambda i: ref.at[i, a], own, x, NX, right_x, left_x, rows_q)

    def ring_z(a, own):
        return gather_ring(links, lambda i: kv.at[i, a], own, z, NZ, right_z, left_z, rows_k)

    def pump(*rings):
        for ring in rings:
            next(ring, None)

    def direct_x(ref, a):
        got = [links.send(ref.at[x, a], ref.at[x, a], seq_dev(mod(x + step, NX), z)) for step in (2, 1, 3)]
        yield
        for n, step in enumerate((2, 1, 3)):
            links.arrived(got[n], ref.at[mod(x - step, NX), a])

    q_a, k_a = direct_x(qg, 0), ring_z(0, kv_own.at[0])
    q_b, k_b = direct_x(qg, 1), ring_z(1, kv.at[z, 1])
    d_a, d_b = ring_x(dg, 0, do_own.at[0]), ring_x(dg, 1, dg.at[x, 1])
    pump(q_a, k_a)
    for load in loads[4:]:
        load.wait()
    for a in range(2):
        rows = nt(wo_v[...], g_v[a * chunk : (a + 1) * chunk, :]).astype(BF16)
        do_own[a] = jnp.concatenate([rows[0:64], rows[64:128]], 1)
    dg[x, 0] = do_own[0]
    links.arrived(sent_q, qg.at[x, 1])
    pump(q_b)
    links.arrived(sent_kv, kv.at[z, 1])
    pump(k_b)
    dkv[...] = jnp.zeros(dkv.shape, F32)
    o_sum[...] = jnp.zeros(o_sum.shape, F32)
    dq_sum[...] = jnp.zeros(dq_sum.shape, F32)
    both[...] = jnp.zeros(both.shape, BF16)
    stats[x, 0] = jnp.full(stats.shape[2:], NEG, F32)
    stats[x, 1] = jnp.zeros(stats.shape[2:], F32)
    def flip(n, _):
        part = pl.ds(pl.multiple_of(n * 128, 128), 128)
        x_t[part, :] = x_v[:, part].astype(F32).T.astype(BF16)
        return 0

    lax.fori_loop(0, x_t.shape[0] // 128, flip, 0)
    pump(q_a)


    def full_tiles(zc):
        tiles = []
        for n in range(3):
            first = n < far_x
            half, block = jnp.where(first, 0, 1), jnp.where(first, x + 1 + n, n + 1)
            tiles += [(half, block, a, zc * 6 + n * 2 + a) for a in range(2)]
        return tiles

    def cross_tiles(zc, a):
        base = 6 * NZ + (0 if a == 0 else 2 * z + 1) + 2 * zc
        return [(0, x, a, base), (1, far_x, a, base + 1)]

    def forward(zc, tiles, cut=()):
        found = []
        for n, (half, block, a, place) in enumerate(tiles):
            s = nn(kv[zc, half][:, 0:64], qg[block, a])
            if n in cut:
                key = lax.broadcasted_iota(jnp.int32, (chunk, lanes), 0)
                row = lax.rem(lax.broadcasted_iota(jnp.int32, (chunk, lanes), 1), chunk)
                on_diagonal = zc == (z if a == 0 else far_z)
                s = jnp.where(row - key >= jnp.where(on_diagonal, 0, -chunk), s, NEG)
            found.append(s)
        highs = [jnp.max(fold(s, jnp.max), axis=0, keepdims=True) for s in found]
        raised = [jnp.exp(s - high) for s, high in zip(found, highs)]
        lows = [p.astype(BF16) for p in raised]
        totals = [jnp.sum(fold(p, jnp.sum), axis=0, keepdims=True) for p in raised]
        for (_, _, _, place), low, high in zip(tiles, lows, highs):
            probs[place] = low
            tops[pl.ds(place, 1), :] = high
        outs = [nn(kvt[zc, half, 64:128, :], low) for (half, _, _, _), low in zip(tiles, lows)]
        for (_, block, a, _), high, total, out in zip(tiles, highs, totals, outs):
            group = pl.ds(block * 2 + a, 1)
            old = stats[x, 0, group, :]
            top = jnp.maximum(old, high)
            keep, add = jnp.exp(old - top), jnp.exp(high - top)
            stats[x, 0, group, :] = top
            stats[x, 1, group, :] = stats[x, 1, group, :] * keep + total * add
            o_sum[block, a] = o_sum[block, a] * keep + out * add

    def flip_slot(zc):
        for half in range(2):
            kvt[zc, half] = kv[zc, half].astype(F32).T.astype(BF16)

    def forward_cross(zc, a):
        if a == 0:
            pl.when(zc < z)(lambda: forward(zc, cross_tiles(zc, 0)))
            pl.when(zc == z)(lambda: forward(zc, cross_tiles(zc, 0)[:1], (0,)))
        else:
            pl.when(zc <= far_z)(lambda: forward(zc, cross_tiles(zc, 1), (1,)))

    def forward_slot(zc):
        flip_slot(zc)
        forward(zc, full_tiles(zc))
        forward_cross(zc, 0)
        forward_cross(zc, 1)

    def slots(work, distances):
        def one(n, _):
            work(mod(z + distances[0] + n * (distances[-1] - distances[0]), NZ))
            return 0

        lax.fori_loop(0, len(distances), one, 0)

    def forward_first(zc):
        flip_slot(zc)
        forward(zc, full_tiles(zc)[0::2])
        forward_cross(zc, 0)

    def forward_second(zc):
        forward(zc, full_tiles(zc)[1::2])
        forward_cross(zc, 1)

    slots(forward_first, (0,))
    pump(k_a, k_b)
    slots(forward_first, (1, -1))
    pump(q_b, d_a)
    sent_do = links.send(do_own.at[1], dg.at[x, 1], mirror_z)
    slots(forward_second, (0,))
    slots(forward_second, (1, -1))
    pump(k_a, k_b)
    slots(forward_slot, (2, -2))
    pump(k_a, k_b, d_a)
    links.arrived(sent_do, dg.at[x, 1])
    pump(d_b)
    slots(forward_slot, (3, -3))
    pump(k_a, k_b, d_a, d_b)
    slots(forward_slot, (4,))
    pump(d_b)

    weights = []
    for step in range(1, NH):
        rows = pl.ds(pl.multiple_of(mod(head + step, NH) * w_all.shape[1], w_all.shape[1]), w_all.shape[1])
        weights.append((links.send(w_cat.at[rows], w_all.at[head], others[step - 1]), step))
    rows = pl.ds(pl.multiple_of(head * w_all.shape[1], w_all.shape[1]), w_all.shape[1])
    w_all[head] = w_cat[rows, :]

    for block in range(NX):
        for a in range(2):
            group = block * 2 + a
            stats[x, 2, group : group + 1, :] = jnp.sum(
                o_sum[block, a] * dg[block, a].astype(F32), axis=0, keepdims=True
            )
    shares = [
        (links.send(stats.at[x], stats.at[x], device), mod(x - step, NX))
        for step, device in ((1, right_x), (2, across_x), (3, left_x))
    ]
    for block in range(NX):
        for a in range(2):
            both[block, 0:64, a * lanes : (a + 1) * lanes] = qg[block, a]
            both[block, 64:128, (2 + a) * lanes : (3 + a) * lanes] = dg[block, a]
    for index, source in shares:
        links.arrived(index, stats.at[source])
    top = functools.reduce(jnp.maximum, [stats[n, 0] for n in range(NX)])
    part = [jnp.exp(stats[n, 0] - top) for n in range(NX)]
    total = sum(stats[n, 1] * part[n] for n in range(NX))
    lse[...] = top + jnp.log(total)
    delta[...] = sum(stats[n, 2] * part[n] for n in range(NX)) / total
    share = jnp.exp(stats[x, 0] - lse[...])
    for block in range(NX):
        for a in range(2):
            group = block * 2 + a
            ring_o[block, a] = (o_sum[block, a] * share[group : group + 1]).astype(BF16)

    def backward_tile(zc, half, block, a, place):
        group = pl.ds(block * 2 + a, 1)
        scale = jnp.exp(tops[pl.ds(place, 1), :] - lse[group, :])
        p = probs[place] * scale.astype(BF16)
        dp = nn(kv[zc, half], both[block, :, (2 + a) * lanes : (3 + a) * lanes])
        return p, p * (dp - delta[group, :]).astype(BF16)

    def backward_full(zc):
        tiles = full_tiles(zc)
        done = [backward_tile(zc, *tile) for tile in tiles]
        for (half, block, a, _), (_, ds) in zip(tiles, done):
            dq_sum[block, a] += nn(kvt[zc, half, 0:64, :], ds)
        for n in range(3):
            half, block = tiles[2 * n][:2]
            (p0, ds0), (p1, ds1) = done[2 * n], done[2 * n + 1]
            dkv[zc, half] += nt(jnp.concatenate([ds0, ds1, p0, p1], 1), both[block])

    def backward_some(zc, tiles):
        done = [backward_tile(zc, *tile) for tile in tiles]
        for (half, block, a, _), (p, ds) in zip(tiles, done):
            dq_sum[block, a] += nn(kvt[zc, half, 0:64, :], ds)
            sides = [both[block, :, n * lanes : (n + 1) * lanes] for n in (a, 2 + a)]
            dkv[zc, half] += nt(jnp.concatenate([ds, p], 1), jnp.concatenate(sides, 1))

    def backward_cross(zc, a):
        if a == 0:
            pl.when(zc < z)(lambda: backward_some(zc, cross_tiles(zc, 0)))
            pl.when(zc == z)(lambda: backward_some(zc, cross_tiles(zc, 0)[:1]))
        else:
            pl.when(zc <= far_z)(lambda: backward_some(zc, cross_tiles(zc, 1)))

    def backward_half(a):
        def work(zc):
            backward_some(zc, full_tiles(zc)[a::2])
            backward_cross(zc, a)

        return work

    def backward_slot(zc):
        backward_full(zc)
        backward_cross(zc, 0)
        backward_cross(zc, 1)

    pair_k = (lambda ref: ref.at[:, 0 : chunk // 2], lambda ref: ref.at[:, chunk // 2 : chunk])

    def home_sums(parts, into, a, back, land, place):
        order = (2, 1, 3)
        got = [
            links.send(parts.at[mod(x + step, NX), a], into.at[x, a], seq_dev(mod(x + step, NX), z))
            for step in order
        ]
        yield
        total = parts[x, a].astype(F32)
        for n, step in enumerate(order):
            source = mod(x - step, NX)
            links.arrived(got[n], into.at[source, a])
            total = total + into[source, a].astype(F32)
        if a == 1:
            back[...] = total.astype(BF16)
            sent = links.send(back, land, mirror_z)
            yield
            links.arrived(sent, land)
            total = land[...].astype(F32)
        place(a, total)

    def keep_in(ref):
        def write(value):
            ref[...] = value.astype(ref.dtype)

        return write

    def token_sums(proj, into, mid, mid_in, write):
        got = [
            links.send(proj.at[mod(x + step, NX)], into.at[x], seq_dev(mod(x + step, NX), z))
            for step in (2, 1, 3)
        ]
        yield
        total = proj[x].astype(F32)
        for n, step in enumerate((2, 1, 3)):
            source = mod(x - step, NX)
            links.arrived(got[n], into.at[source])
            total = total + into[source].astype(F32)
        mid[...] = total.astype(BF16)
        order = (4, 3, 5, 2, 6, 1, 7)
        got = [
            links.send(mid.at[mod(z + step, NZ)], mid_in.at[z], seq_dev(x, mod(z + step, NZ)))
            for step in order
        ]
        yield
        total = mid[z].astype(F32)
        for n, step in enumerate(order):
            source = mod(z - step, NZ)
            links.arrived(got[n], mid_in.at[source])
            total = total + mid_in[source].astype(F32)
        write(total)

    def token_sums_zx(proj, into, mid, mid_in, write):
        order = (4, 3, 5, 2, 6, 1, 7)
        got = [
            links.send(proj.at[:, mod(z + step, NZ)], into.at[z], seq_dev(x, mod(z + step, NZ)))
            for step in order
        ]
        yield
        total = proj[:, z].astype(F32)
        for n, step in enumerate(order):
            source = mod(z - step, NZ)
            links.arrived(got[n], into.at[source])
            total = total + into[source].astype(F32)
        mid[...] = total.astype(BF16)
        got = [
            links.send(mid.at[mod(x + step, NX)], mid_in.at[x], seq_dev(mod(x + step, NX), z))
            for step in (2, 1, 3)
        ]
        yield
        total = mid[x].astype(F32)
        for n, step in enumerate((2, 1, 3)):
            source = mod(x - step, NX)
            links.arrived(got[n], mid_in.at[source])
            total = total + mid_in[source].astype(F32)
        write(total)

    def spread(part):
        rows = g_t.shape[1] // 2
        cut = (lambda ref: ref.at[0:rows], lambda ref: ref.at[rows : 2 * rows])

        def slot(i, c):
            return g_all.at[i * 2 + c, part]

        own = g_t.at[part]
        ring = gather_ring(links, lambda i: slot(i, core), own, y, 4, right_y, left_y, cut)
        next(ring)
        got = [(links.send(own, slot(y, core), twin), y)]
        g_all[head, part] = g_t[part]
        yield
        next(ring)
        for i in (mod(y - 1, 4), mod(y + 1, 4)):
            got.append((links.send(slot(i, core), slot(i, core), twin), i))
        yield
        for _ in ring:
            pass
        i = mod(y + 2, 4)
        got.append((links.send(slot(i, core), slot(i, core), twin), i))
        yield
        for index, i in got:
            links.arrived(index, slot(i, 1 - core))

    def project(proj, rows):
        def one(i, _):
            part = pl.ds(pl.multiple_of(i * 512, 512), 512)
            proj[i] = nt(x_t[part, :], rows[...]).astype(BF16).reshape(proj.shape[1:])
            return 0

        lax.fori_loop(0, NX, one, 0)

    def write_kv(value):
        gk_out[...] = value[:, 0:64]
        gv_out[...] = value[:, 64:128]

    kv_home = []

    def finish_kv(value):
        kv_home.append(value[0])
        dkv_back[...] = value[1].astype(BF16)
        kv_home.append(links.send(dkv_back, dkv_land, mirror_x))

    kv_ring = scatter_ring(links, lambda i: dkv.at[i], lambda i: dkv_snd.at[i], lambda i: dkv_l.at[i],
                           lambda i: dkv_r.at[i], z, NZ, right_z, left_z, pair_k, finish_kv)
    def place_o(a, rows):
        for h in range(2):
            o_t[h * 64 : (h + 1) * 64, a * chunk : (a + 1) * chunk] = rows[
                :, h * chunk : (h + 1) * chunk
            ].astype(BF16)

    def place_q(a, rows):
        for h in range(2):
            g_t[0, h * 64 : (h + 1) * 64, a * chunk : (a + 1) * chunk] = turn(
                rows[:, h * chunk : (h + 1) * chunk], a, -1.0
            ).astype(BF16)

    def place_kv(a, rows):
        columns = slice(a * chunk, (a + 1) * chunk)
        g_t[1, 0:64, columns] = turn(rows[0:64], a, -1.0).astype(BF16)
        g_t[1, 64:128, columns] = rows[64:128].astype(BF16)

    def project_o(i, _):
        part = pl.ds(pl.multiple_of(i * 512, 512), 512)
        proj_o[i] = nn(o_t[...], g_v[:, part]).T.astype(BF16).reshape(proj_o.shape[1:])
        return 0

    o_home, o_home_far = (home_sums(ring_o, o_in, a, o_back, o_land, place_o) for a in range(2))
    q_home, q_home_far = (home_sums(ring_q, q_in, a, q_back, q_land, place_q) for a in range(2))
    o_proj = token_sums(proj_o, po_in, po_mid, po_mid_in, keep_in(go_out))
    kv_proj = token_sums_zx(proj_kv, pk_in, pk_mid, pk_mid_in, write_kv)
    q_proj = token_sums(proj_q, pq_in, pq_mid, pq_mid_in, keep_in(gq_out))
    gather_q, gather_kv = spread(0), spread(1)

    def pack_q(a):
        for block in range(NX):
            ring_q[block, a] = (dq_sum[block, a] * 0.125).astype(BF16)

    pump(o_home_far, o_home)
    slots(backward_slot, (4,))
    pump(kv_ring)
    slots(backward_slot, (3, -3))
    pump(kv_ring, o_home_far, o_home)
    slots(backward_slot, (2, -2))
    pump(kv_ring, o_home_far)
    lax.fori_loop(0, NX, project_o, 0)
    pump(o_proj)
    slots(backward_half(1), (1, -1))
    slots(backward_half(1), (0,))
    pack_q(1)
    pump(q_home_far)
    slots(backward_half(0), (1, -1))
    pump(kv_ring, o_proj)
    slots(backward_half(0), (0,))
    pack_q(0)
    pump(q_home, q_home_far, kv_ring)
    place_kv(0, kv_home[0].T)
    links.arrived(kv_home[1], dkv_land)
    place_kv(1, dkv_land[...].astype(F32).T)
    pump(gather_kv)
    project(proj_kv, g_t.at[1])
    pump(kv_proj, q_home, q_home_far, gather_q)
    project(proj_q, g_t.at[0])
    pump(q_proj, gather_kv, gather_q, gather_kv, gather_q, gather_kv)
    for index, step in weights:
        links.arrived(index, w_all.at[mod(head - step, NH)])
    gi_sum[...] = sum(nn(w_all[n, :, 128:256], g_all[n, 1]) for n in range(NH))
    pump(gather_q, q_proj)
    total = gi_sum[...] + sum(nn(w_all[n, :, 0:128], g_all[n, 0]) for n in range(NH))
    gi_out[...] = total.T.astype(BF16)
    pump(kv_proj)
    together(q_proj, kv_proj, o_proj)
    links.drain()


def layer(inputs, out_grad, w_query, w_key, w_value, w_output, cos_t, sin_t):
    tokens, model = inputs.shape
    chunk, lanes = tokens // 2, tokens
    slab = model // (NX * NZ)
    tiles = (2 * NX * 2 * NZ) // 2 + 1
    vmem = pl.BlockSpec(memory_space=pltpu.VMEM)
    anywhere = pl.BlockSpec(memory_space=pl.ANY)
    copies = 120

    def vm(*shape, dtype=BF16):
        return pltpu.VMEM(shape, dtype)

    rows = (NX, 2, 64, lanes)

    sums = [vm(NX, NZ, slab, 128), vm(NX, NZ, slab, 128), vm(NZ, slab, 128), vm(NZ, slab, 128)]
    return pl.pallas_call(
        layer_kernel,
        out_shape=(
            jax.ShapeDtypeStruct((tokens, 256), BF16),
            jax.ShapeDtypeStruct((slab, 128), F32),
            jax.ShapeDtypeStruct((slab, 64), F32),
            jax.ShapeDtypeStruct((slab, 64), F32),
            jax.ShapeDtypeStruct((slab, 128), F32),
        ),
        in_specs=[anywhere] * 6 + [vmem] * 2,
        out_specs=(vmem,) * 5,
        scratch_shapes=[
            vm(tokens, model), vm(tokens, model), vm(model, 256), vm(64, model), vm(64, model), vm(128, model),
            vm(NH, model // NH, 256), vm(model, tokens),
            vm(2, 64, lanes), vm(2, 64, lanes), vm(2, chunk, 128),
            vm(*rows), vm(*rows), vm(NZ, 2, chunk, 128), vm(NZ, 2, 128, chunk), vm(NX, 128, 4 * lanes),
            vm(tiles, chunk, lanes), vm(tiles + 7, lanes, dtype=F32), vm(NX, 3, 8, lanes, dtype=F32),
            vm(8, lanes, dtype=F32), vm(8, lanes, dtype=F32), vm(*rows, dtype=F32), vm(*rows, dtype=F32),
            vm(NZ, 2, chunk, 128, dtype=F32),
            vm(*rows), vm(*rows), vm(64, lanes), vm(64, lanes), vm(*rows), vm(*rows), vm(64, lanes), vm(64, lanes),
            vm(128, tokens), vm(2, 128, tokens),
            vm(NZ, 2, chunk, 128), vm(NZ // 2, 2, chunk, 128), vm(NZ // 2, 2, chunk, 128),
            vm(chunk, 128), vm(chunk, 128),
        ] + sums + [
            vm(NX, NZ, slab, 128), vm(NZ, NX, slab, 128), vm(NX, slab, 128), vm(NX, slab, 128),
        ] + sums + [
            vm(NH, 2, 128, tokens), vm(256, tokens, dtype=F32),
            pltpu.SemaphoreType.DMA((copies,)),
            pltpu.SemaphoreType.DMA((copies,)),
            pltpu.SemaphoreType.DMA((6,)),
        ],
        compiler_params=pltpu.CompilerParams(
            collective_id=0, has_side_effects=True, vmem_limit_bytes=60 * 1024 * 1024
        ),
        name="layer",
    )(inputs, out_grad, w_query, w_key, w_value, w_output, cos_t, sin_t)


def hand_on_kernel(*refs):
    count = len(refs) // 2
    for source, target in zip(refs[:count], refs[count:]):
        target[...] = source[...]


def hand_on(arrays):
    vmem = pl.BlockSpec(memory_space=pltpu.VMEM)
    return pl.pallas_call(
        hand_on_kernel,
        out_shape=tuple(jax.ShapeDtypeStruct(array.shape, array.dtype) for array in arrays),
        in_specs=[vmem] * len(arrays),
        out_specs=(vmem,) * len(arrays),
        name="hand_on",
    )(*arrays)


def body(inputs, out_grad, w_query, w_key, w_value, w_output):
    tokens = inputs.shape[0]
    me = lax.axis_index("seq")
    positions = (me * tokens + jnp.arange(tokens, dtype=jnp.int32)).astype(F32)
    cos, sin = rotary(positions)
    results = layer(inputs, out_grad, w_query, w_key.T, w_value.T, w_output, cos.T, sin.T)
    *grads, grad_output = hand_on(results)
    return (*grads, grad_output.T)


def solution(mesh):
    placed = (
        P("seq", None),
        P("seq", None),
        P(None, "head"),
        P(None, "head"),
        P(None, "head"),
        P("head", None),
    )
    return jax.shard_map(
        body,
        mesh=mesh,
        in_specs=placed,
        out_specs=(
            P("seq", "head"),
            P("seq", "head"),
            P("seq", "head"),
            P("seq", "head"),
            P("head", "seq"),
        ),
        check_vma=False,
    )
```

```python
import functools

import jax
import jax.numpy as jnp
from jax import lax
from jax.experimental import pallas as pl
from jax.experimental.pallas import tpu as pltpu
from jax.sharding import PartitionSpec as P

HD = 64
NX, NZ, NH = 4, 8, 8
ROPE_BASE = 500000.0
NEG = -1e30
F32, BF16 = jnp.float32, jnp.bfloat16
MESH = pl.DeviceIdType.MESH


def rotary(positions):
    half_dim = HD // 2
    frequency = ROPE_BASE ** (-(jnp.arange(half_dim, dtype=jnp.float32) * 2.0 / HD))
    angles = positions[:, None] * frequency[None, :]
    return jnp.cos(angles), jnp.sin(angles)


def mod(value, size):
    return lax.rem(value + 2 * size, size)


class Links:
    def __init__(self, send_sems, recv_sems):
        self.send_sems, self.recv_sems = send_sems, recv_sems
        self.used, self.open = 0, []

    def send(self, src, dst, device):
        index = self.used
        self.used += 1
        copy = pltpu.make_async_remote_copy(
            src_ref=src,
            dst_ref=dst,
            send_sem=self.send_sems.at[index],
            recv_sem=self.recv_sems.at[index],
            device_id=device,
            device_id_type=MESH,
        )
        copy.start()
        self.open.append(copy)
        return index

    def arrived(self, index, landing):
        pltpu.make_async_copy(landing, landing, self.recv_sems.at[index]).wait()

    def drain(self):
        for copy in self.open:
            copy.wait_send()
        self.open = []


def together(*streams):
    streams = list(streams)
    while streams:
        for stream in list(streams):
            try:
                next(stream)
            except StopIteration:
                streams.remove(stream)


def gather_ring(links, slots, own, where, size, right, left, cut):
    far = size // 2
    low, high = cut
    held_r, held_l = own, own
    for step in range(1, far + 1):
        slot_r, slot_l = mod(where - step + 1, size), mod(where + step - 1, size)
        if step == far:
            held_r, held_l = low(held_r), high(held_l)
            place_r, place_l = low(slots(slot_r)), high(slots(slot_l))
        else:
            place_r, place_l = slots(slot_r), slots(slot_l)
        got_r = links.send(held_r, place_r, right)
        got_l = links.send(held_l, place_l, left)
        yield
        held_r, held_l = slots(mod(where - step, size)), slots(mod(where + step, size))
        if step == far:
            links.arrived(got_r, low(held_r))
            links.arrived(got_l, high(held_l))
        else:
            links.arrived(got_r, held_r)
            links.arrived(got_l, held_l)


def scatter_ring(links, mine, snd, from_left, from_right, where, size, right, left, cut, finish):
    far = size // 2
    low, high = cut
    owner = mod(where + far, size)
    snd(owner)[...] = mine(owner)[...].astype(BF16)
    got_r = links.send(low(snd(owner)), low(from_left(0)), right)
    got_l = links.send(high(snd(owner)), high(from_right(0)), left)
    for step in range(2, far + 1):
        yield
        for got, came, place, sign, part, target in (
            (got_r, from_left, from_left, 1, low, right),
            (got_l, from_right, from_right, -1, high, left),
        ):
            owner = mod(where + sign * (far - step + 1), size)
            if step == 2:
                links.arrived(got, part(came(0)))
                other = high if part is low else low
                part(snd(owner))[...] = (
                    part(mine(owner))[...].astype(F32) + part(came(0))[...].astype(F32)
                ).astype(BF16)
                other(snd(owner))[...] = other(mine(owner))[...].astype(BF16)
            else:
                links.arrived(got, came(step - 2))
                snd(owner)[...] = (
                    mine(owner)[...].astype(F32) + came(step - 2)[...].astype(F32)
                ).astype(BF16)
            sent = links.send(snd(owner), place(step - 1), target)
            if sign == 1:
                got_r = sent
            else:
                got_l = sent
    yield
    links.arrived(got_r, from_left(far - 1))
    links.arrived(got_l, from_right(far - 1))
    finish(
        mine(where)[...].astype(F32)
        + from_left(far - 1)[...].astype(F32)
        + from_right(far - 1)[...].astype(F32)
    )


def seq_place():
    me = lax.axis_index("seq")
    return lax.div(me, NZ), lax.rem(me, NZ)


def seq_dev(x, z):
    return {"seq": x * NZ + z}


def nn(a, b):
    return lax.dot_general(a, b, (((1,), (0,)), ((), ())), preferred_element_type=F32)


def nt(a, b):
    return lax.dot_general(a, b, (((1,), (1,)), ((), ())), preferred_element_type=F32)


def fold(values, op):
    return op(values.reshape(values.shape[0] // 8, 8, values.shape[1]), axis=0)


def layer_kernel(
    inputs, out_grad, w_query, w_key, w_value, w_output, cos_t, sin_t,
    gi_out, gq_out, gk_out, gv_out, go_out,
    x_v, g_v, w_cat, wk_v, wv_v, wo_v, w_all, x_t,
    q_own, do_own, kv_own,
    qg, dg, kv, kvt, both, probs, tops, stats, lse, delta, o_sum, dq_sum, dkv,
    ring_o, o_in, o_back, o_land, ring_q, q_in, q_back, q_land, o_t, g_t,
    dkv_snd, dkv_l, dkv_r, dkv_back, dkv_land,
    proj_o, po_in, po_mid, po_mid_in,
    proj_kv, pk_in, pk_mid, pk_mid_in,
    proj_q, pq_in, pq_mid, pq_mid_in,
    g_all, gi_sum,
    send_sems, recv_sems, copy_sems,
):
    x, z = seq_place()
    head = lax.axis_index("head")
    y, core = lax.div(head, 2), lax.rem(head, 2)
    chunk, lanes = kv_own.shape[1], q_own.shape[2]
    far_x, far_z = NX - 1 - x, NZ - 1 - z
    right_x, left_x = seq_dev(mod(x + 1, NX), z), seq_dev(mod(x - 1, NX), z)
    across_x, mirror_x = seq_dev(mod(x + 2, NX), z), seq_dev(far_x, z)
    right_z, left_z = seq_dev(x, mod(z + 1, NZ)), seq_dev(x, mod(z - 1, NZ))
    mirror_z = seq_dev(x, far_z)
    others = [{"head": mod(head + step, NH)} for step in range(1, NH)]
    right_y, left_y = {"head": mod(y + 1, 4) * 2 + core}, {"head": mod(y - 1, 4) * 2 + core}
    twin = {"head": y * 2 + 1 - core}

    loads = [
        pltpu.make_async_copy(source, target, copy_sems.at[n])
        for n, (source, target) in enumerate(
            (
                (w_query, w_cat.at[:, 0:128]),
                (w_key, wk_v),
                (w_value, wv_v),
                (inputs, x_v),
                (w_output, wo_v),
                (out_grad, g_v),
            )
        )
    ]
    for load in loads:
        load.start()
    partners = (
        [seq_dev(mod(x + step, NX), z) for step in range(1, NX)]
        + [seq_dev(x, mod(z + step, NZ)) for step in range(1, NZ)]
        + others
    )
    barrier = pltpu.get_barrier_semaphore()
    for device in partners:
        pl.semaphore_signal(barrier, inc=1, device_id=device, device_id_type=MESH)
    links = Links(send_sems, recv_sems)

    for load in loads[:3]:
        load.wait()
    w_kv = jnp.concatenate([wk_v[...], wv_v[...]], 0)
    w_cat[:, 128:256] = w_kv.astype(F32).T.astype(BF16)
    loads[3].wait()

    def turn(rows, a, sign):
        cos, sin = (table[:, a * chunk : (a + 1) * chunk] for table in (cos_t, sin_t))
        front, back = rows[0:32], rows[32:64]
        return jnp.concatenate([front * cos - sign * back * sin, back * cos + sign * front * sin], 0)

    for a in range(2):
        rows = nn(x_v[a * chunk : (a + 1) * chunk, :], w_cat[...]).T
        q = jnp.concatenate([turn(rows[0:64], a, 1.0), turn(rows[64:128], a, 1.0)], 1).astype(BF16)
        q_own[a] = q * jnp.asarray(0.125, BF16)
        kv_own[a] = jnp.concatenate([turn(rows[128:192], a, 1.0), rows[192:256]], 0).T.astype(BF16)
    qg[x, 0] = q_own[0]
    kv[z, 0] = kv_own[0]
    pl.semaphore_wait(barrier, len(partners))

    sent_q = links.send(q_own.at[1], qg.at[x, 1], mirror_z)
    sent_kv = links.send(kv_own.at[1], kv.at[z, 1], mirror_x)
    rows_k = (lambda ref: ref.at[0 : chunk // 2], lambda ref: ref.at[chunk // 2 : chunk])

    def ring_z(a, own):
        return gather_ring(links, lambda i: kv.at[i, a], own, z, NZ, right_z, left_z, rows_k)

    def pump(*rings):
        for ring in rings:
            next(ring, None)

    def direct_x(ref, a):
        got = [links.send(ref.at[x, a], ref.at[x, a], seq_dev(mod(x + step, NX), z)) for step in (2, 1, 3)]
        yield
        for n, step in enumerate((2, 1, 3)):
            links.arrived(got[n], ref.at[mod(x - step, NX), a])

    q_a, k_a = direct_x(qg, 0), ring_z(0, kv_own.at[0])
    q_b, k_b = direct_x(qg, 1), ring_z(1, kv.at[z, 1])
    d_a, d_b = direct_x(dg, 0), direct_x(dg, 1)
    pump(q_a, k_a)
    for load in loads[4:]:
        load.wait()
    for a in range(2):
        rows = nt(wo_v[...], g_v[a * chunk : (a + 1) * chunk, :]).astype(BF16)
        do_own[a] = jnp.concatenate([rows[0:64], rows[64:128]], 1)
    dg[x, 0] = do_own[0]
    links.arrived(sent_q, qg.at[x, 1])
    pump(q_b)
    links.arrived(sent_kv, kv.at[z, 1])
    pump(k_b)
    dkv[...] = jnp.zeros(dkv.shape, F32)
    o_sum[...] = jnp.zeros(o_sum.shape, F32)
    dq_sum[...] = jnp.zeros(dq_sum.shape, F32)
    both[...] = jnp.zeros(both.shape, BF16)
    for a in range(2):
        place = lax.broadcasted_iota(jnp.int32, stats.shape[2:], 0)
        stats[x, a] = jnp.where(place < NX, NEG, 0.0)
    def flip(n, _):
        part = pl.ds(pl.multiple_of(n * 128, 128), 128)
        x_t[part, :] = x_v[:, part].astype(F32).T.astype(BF16)
        return 0

    lax.fori_loop(0, x_t.shape[0] // 128, flip, 0)
    pump(q_a)


    def full_tiles(zc):
        tiles = []
        for n in range(3):
            first = n < far_x
            half, block = jnp.where(first, 0, 1), jnp.where(first, x + 1 + n, n + 1)
            tiles += [(half, block, a, zc * 6 + n * 2 + a) for a in range(2)]
        return tiles

    def cross_tiles(zc, a):
        base = 6 * NZ + (0 if a == 0 else 2 * z + 1) + 2 * zc
        return [(0, x, a, base), (1, far_x, a, base + 1)]

    def forward(zc, tiles, cut=()):
        found = []
        for n, (half, block, a, place) in enumerate(tiles):
            s = nn(kv[zc, half][:, 0:64], qg[block, a])
            if n in cut:
                key = lax.broadcasted_iota(jnp.int32, (chunk, lanes), 0)
                row = lax.rem(lax.broadcasted_iota(jnp.int32, (chunk, lanes), 1), chunk)
                on_diagonal = zc == (z if a == 0 else far_z)
                s = jnp.where(row - key >= jnp.where(on_diagonal, 0, -chunk), s, NEG)
            found.append(s)
        highs = [jnp.max(fold(s, jnp.max), axis=0, keepdims=True) for s in found]
        raised = [jnp.exp(s - high) for s, high in zip(found, highs)]
        lows = [p.astype(BF16) for p in raised]
        for (_, _, _, place), low, high in zip(tiles, lows, highs):
            probs[place] = low
            tops[pl.ds(place, 1), :] = high
        outs = [nn(kvt[zc, half, 64:144, :], low) for (half, _, _, _), low in zip(tiles, lows)]
        for (_, block, a, _), high, out in zip(tiles, highs, outs):
            top_row, sum_row = pl.ds(block, 1), pl.ds(NX + block, 1)
            old = stats[x, a, top_row, :]
            top = jnp.maximum(old, high)
            keep, add = jnp.exp(old - top), jnp.exp(high - top)
            stats[x, a, top_row, :] = top
            stats[x, a, sum_row, :] = stats[x, a, sum_row, :] * keep + out[64:65] * add
            o_sum[block, a] = o_sum[block, a] * keep + out[0:64] * add

    def flip_slot(zc):
        for half in range(2):
            kvt[zc, half, 0:128, :] = kv[zc, half].astype(F32).T.astype(BF16)
            kvt[zc, half, 128:144, :] = jnp.ones((16, chunk), BF16)

    def forward_cross(zc, a):
        if a == 0:
            pl.when(zc < z)(lambda: forward(zc, cross_tiles(zc, 0)))
            pl.when(zc == z)(lambda: forward(zc, cross_tiles(zc, 0)[:1], (0,)))
        else:
            pl.when(zc <= far_z)(lambda: forward(zc, cross_tiles(zc, 1), (1,)))

    def forward_slot(zc):
        flip_slot(zc)
        forward(zc, full_tiles(zc))
        forward_cross(zc, 0)
        forward_cross(zc, 1)

    def slots(work, distances):
        def one(n, _):
            work(mod(z + distances[0] + n * (distances[-1] - distances[0]), NZ))
            return 0

        lax.fori_loop(0, len(distances), one, 0)

    def forward_first(zc):
        flip_slot(zc)
        forward(zc, full_tiles(zc)[0::2])
        forward_cross(zc, 0)

    def forward_second(zc):
        forward(zc, full_tiles(zc)[1::2])
        forward_cross(zc, 1)

    slots(forward_first, (0,))
    pump(k_a, k_b)
    slots(forward_first, (1, -1))
    pump(q_b, d_a)
    sent_do = links.send(do_own.at[1], dg.at[x, 1], mirror_z)
    slots(forward_second, (0,))
    slots(forward_second, (1, -1))
    pump(k_a, k_b)
    slots(forward_slot, (2, -2))
    pump(k_a, k_b)
    links.arrived(sent_do, dg.at[x, 1])
    pump(d_b)
    slots(forward_slot, (3, -3))
    pump(k_a, k_b, d_a)
    last = mod(z + NZ // 2, NZ)

    def share_stats(a):
        for block in range(NX):
            stats[x, a, 2 * NX + block : 2 * NX + block + 1, :] = jnp.sum(
                o_sum[block, a] * dg[block, a].astype(F32), axis=0, keepdims=True
            )
        return [
            (links.send(stats.at[x, a], stats.at[x, a], device), mod(x - step, NX))
            for step, device in ((2, across_x), (1, right_x), (3, left_x))
        ]

    def settle(a, shares):
        for index, source in shares:
            links.arrived(index, stats.at[source, a])
        top = functools.reduce(jnp.maximum, [stats[n, a, 0:NX, :] for n in range(NX)])
        part = [jnp.exp(stats[n, a, 0:NX, :] - top) for n in range(NX)]
        total = sum(stats[n, a, NX : 2 * NX, :] * part[n] for n in range(NX))
        level = top + jnp.log(total)
        lse[a * NX : (a + 1) * NX, :] = level
        delta[a * NX : (a + 1) * NX, :] = (
            sum(stats[n, a, 2 * NX : 3 * NX, :] * part[n] for n in range(NX)) / total
        )
        share = jnp.exp(stats[x, a, 0:NX, :] - level)
        for block in range(NX):
            ring_o[block, a] = (o_sum[block, a] * share[block : block + 1]).astype(BF16)

    flip_slot(last)
    forward_second(last)
    pump(d_b)
    shares_far = share_stats(1)
    forward(last, full_tiles(last)[0::2])
    forward_cross(last, 0)
    shares_near = share_stats(0)
    for block in range(NX):
        for a in range(2):
            both[block, a, 0:64, 0:lanes] = qg[block, a]
            both[block, a, 64:128, lanes : 2 * lanes] = dg[block, a]

    weights = []
    for step in range(1, NH):
        rows = pl.ds(pl.multiple_of(mod(head + step, NH) * w_all.shape[1], w_all.shape[1]), w_all.shape[1])
        weights.append((links.send(w_cat.at[rows], w_all.at[head], others[step - 1]), step))
    rows = pl.ds(pl.multiple_of(head * w_all.shape[1], w_all.shape[1]), w_all.shape[1])
    w_all[head] = w_cat[rows, :]

    def backward_tile(zc, half, block, a, place):
        group = pl.ds(a * NX + block, 1)
        scale = jnp.exp(tops[pl.ds(place, 1), :] - lse[group, :])
        p = probs[place] * scale.astype(BF16)
        dp = nn(kv[zc, half], both[block, a, :, lanes : 2 * lanes])
        return p, p * (dp - delta[group, :]).astype(BF16)

    def backward_tiles(columns):
        done = [[backward_tile(zc, *tile) for tile in tiles] for zc, tiles in columns]
        for n, (half, block, a, _) in enumerate(columns[0][1]):
            keys = [kvt[zc, half, 0:64, :] for zc, _ in columns]
            ds = [pairs[n][1] for pairs in done]
            if len(columns) == 1:
                dq_sum[block, a] += nn(keys[0], ds[0])
            else:
                dq_sum[block, a] += nn(jnp.concatenate(keys, 1), jnp.concatenate(ds, 0))
        for (zc, tiles), pairs in zip(columns, done):
            for (half, block, a, _), (p, ds) in zip(tiles, pairs):
                dkv[zc, half] += nt(jnp.concatenate([ds, p], 1), both[block, a])

    def backward_cross(zc, a):
        if a == 0:
            pl.when(zc < z)(lambda: backward_tiles([(zc, cross_tiles(zc, 0))]))
            pl.when(zc == z)(lambda: backward_tiles([(zc, cross_tiles(zc, 0)[:1])]))
        else:
            pl.when(zc <= far_z)(lambda: backward_tiles([(zc, cross_tiles(zc, 1))]))

    def backward(distances, a):
        places = [mod(z + distance, NZ) for distance in distances]
        backward_tiles([(zc, full_tiles(zc)[a::2]) for zc in places])
        slots(lambda zc: backward_cross(zc, a), distances)

    pair_k = (lambda ref: ref.at[:, 0 : chunk // 2], lambda ref: ref.at[:, chunk // 2 : chunk])

    def home_sums(parts, into, a, back, land, place):
        order = (2, 1, 3)
        got = [
            links.send(parts.at[mod(x + step, NX), a], into.at[x, a], seq_dev(mod(x + step, NX), z))
            for step in order
        ]
        yield
        total = parts[x, a].astype(F32)
        for n, step in enumerate(order):
            source = mod(x - step, NX)
            links.arrived(got[n], into.at[source, a])
            total = total + into[source, a].astype(F32)
        if a == 1:
            back[...] = total.astype(BF16)
            sent = links.send(back, land, mirror_z)
            yield
            links.arrived(sent, land)
            total = land[...].astype(F32)
        place(a, total)

    def keep_in(ref):
        def write(value):
            ref[...] = value.astype(ref.dtype)

        return write

    def token_sums(proj, into, mid, mid_in, write):
        got = [
            links.send(proj.at[mod(x + step, NX)], into.at[x], seq_dev(mod(x + step, NX), z))
            for step in (2, 1, 3)
        ]
        yield
        total = proj[x].astype(F32)
        for n, step in enumerate((2, 1, 3)):
            source = mod(x - step, NX)
            links.arrived(got[n], into.at[source])
            total = total + into[source].astype(F32)
        mid[...] = total.astype(BF16)
        order = (4, 3, 5, 2, 6, 1, 7)
        got = [
            links.send(mid.at[mod(z + step, NZ)], mid_in.at[z], seq_dev(x, mod(z + step, NZ)))
            for step in order
        ]
        yield
        total = mid[z].astype(F32)
        for n, step in enumerate(order):
            source = mod(z - step, NZ)
            links.arrived(got[n], mid_in.at[source])
            total = total + mid_in[source].astype(F32)
        write(total)

    def token_sums_zx(proj, into, mid, mid_in, write):
        order = (4, 3, 5, 2, 6, 1, 7)
        got = [
            links.send(proj.at[:, mod(z + step, NZ)], into.at[z], seq_dev(x, mod(z + step, NZ)))
            for step in order
        ]
        yield
        total = proj[:, z].astype(F32)
        for n, step in enumerate(order):
            source = mod(z - step, NZ)
            links.arrived(got[n], into.at[source])
            total = total + into[source].astype(F32)
        mid[...] = total.astype(BF16)
        got = [
            links.send(mid.at[mod(x + step, NX)], mid_in.at[x], seq_dev(mod(x + step, NX), z))
            for step in (2, 1, 3)
        ]
        yield
        total = mid[x].astype(F32)
        for n, step in enumerate((2, 1, 3)):
            source = mod(x - step, NX)
            links.arrived(got[n], mid_in.at[source])
            total = total + mid_in[source].astype(F32)
        write(total)

    def spread(part):
        rows = g_t.shape[1] // 2
        cut = (lambda ref: ref.at[0:rows], lambda ref: ref.at[rows : 2 * rows])

        def slot(i, c):
            return g_all.at[i * 2 + c, part]

        own = g_t.at[part]
        ring = gather_ring(links, lambda i: slot(i, core), own, y, 4, right_y, left_y, cut)
        next(ring)
        got = [(links.send(own, slot(y, core), twin), y)]
        g_all[head, part] = g_t[part]
        yield
        next(ring)
        for i in (mod(y - 1, 4), mod(y + 1, 4)):
            got.append((links.send(slot(i, core), slot(i, core), twin), i))
        yield
        for _ in ring:
            pass
        i = mod(y + 2, 4)
        got.append((links.send(slot(i, core), slot(i, core), twin), i))
        yield
        for index, i in got:
            links.arrived(index, slot(i, 1 - core))

    def project(proj, rows):
        def one(i, _):
            part = pl.ds(pl.multiple_of(i * 512, 512), 512)
            proj[i] = nt(x_t[part, :], rows[...]).astype(BF16).reshape(proj.shape[1:])
            return 0

        lax.fori_loop(0, NX, one, 0)

    def write_kv(value):
        gk_out[...] = value[:, 0:64]
        gv_out[...] = value[:, 64:128]

    kv_home = []

    def finish_kv(value):
        kv_home.append(value[0])
        dkv_back[...] = value[1].astype(BF16)
        kv_home.append(links.send(dkv_back, dkv_land, mirror_x))

    kv_ring = scatter_ring(links, lambda i: dkv.at[i], lambda i: dkv_snd.at[i], lambda i: dkv_l.at[i],
                           lambda i: dkv_r.at[i], z, NZ, right_z, left_z, pair_k, finish_kv)
    def place_o(a, rows):
        for h in range(2):
            o_t[h * 64 : (h + 1) * 64, a * chunk : (a + 1) * chunk] = rows[
                :, h * chunk : (h + 1) * chunk
            ].astype(BF16)

    def place_q(a, rows):
        for h in range(2):
            g_t[0, h * 64 : (h + 1) * 64, a * chunk : (a + 1) * chunk] = turn(
                rows[:, h * chunk : (h + 1) * chunk], a, -1.0
            ).astype(BF16)

    def place_kv(a, rows):
        columns = slice(a * chunk, (a + 1) * chunk)
        g_t[1, 0:64, columns] = turn(rows[0:64], a, -1.0).astype(BF16)
        g_t[1, 64:128, columns] = rows[64:128].astype(BF16)

    def project_o(i, _):
        part = pl.ds(pl.multiple_of(i * 512, 512), 512)
        proj_o[i] = nn(o_t[...], g_v[:, part]).T.astype(BF16).reshape(proj_o.shape[1:])
        return 0

    o_home, o_home_far = (home_sums(ring_o, o_in, a, o_back, o_land, place_o) for a in range(2))
    q_home, q_home_far = (home_sums(ring_q, q_in, a, q_back, q_land, place_q) for a in range(2))
    o_proj = token_sums(proj_o, po_in, po_mid, po_mid_in, keep_in(go_out))
    kv_proj = token_sums_zx(proj_kv, pk_in, pk_mid, pk_mid_in, write_kv)
    q_proj = token_sums(proj_q, pq_in, pq_mid, pq_mid_in, keep_in(gq_out))
    gather_q, gather_kv = spread(0), spread(1)

    def pack_q(a):
        for block in range(NX):
            ring_q[block, a] = (dq_sum[block, a] * 0.125).astype(BF16)

    settle(1, shares_far)
    pump(o_home_far)
    backward((4,), 1)
    settle(0, shares_near)
    pump(o_home)
    backward((4,), 0)
    pump(kv_ring)
    backward((3, -3), 1)
    pump(o_home_far)
    backward((3, -3), 0)
    pump(kv_ring, o_home)
    backward((2, -2), 1)
    pump(o_home_far)
    lax.fori_loop(0, NX, project_o, 0)
    pump(o_proj)
    backward((2, -2), 0)
    pump(kv_ring)
    backward((1, -1), 1)
    backward((1, -1), 0)
    pump(kv_ring)
    backward((0,), 1)
    pack_q(1)
    pump(q_home_far, o_proj)
    backward((0,), 0)
    pack_q(0)
    pump(q_home, kv_ring, q_home_far)
    place_kv(0, kv_home[0].T)
    links.arrived(kv_home[1], dkv_land)
    place_kv(1, dkv_land[...].astype(F32).T)
    pump(gather_kv)
    project(proj_kv, g_t.at[1])
    pump(kv_proj, q_home, q_home_far, gather_q)
    project(proj_q, g_t.at[0])
    pump(q_proj, gather_kv, gather_q, gather_kv, gather_q, gather_kv)
    for index, step in weights:
        links.arrived(index, w_all.at[mod(head - step, NH)])
    gi_sum[...] = sum(nn(w_all[n, :, 128:256], g_all[n, 1]) for n in range(NH))
    pump(gather_q, q_proj)
    total = gi_sum[...] + sum(nn(w_all[n, :, 0:128], g_all[n, 0]) for n in range(NH))
    gi_out[...] = total.T.astype(BF16)
    pump(kv_proj)
    together(q_proj, kv_proj, o_proj)
    links.drain()


def layer(inputs, out_grad, w_query, w_key, w_value, w_output, cos_t, sin_t):
    tokens, model = inputs.shape
    chunk, lanes = tokens // 2, tokens
    slab = model // (NX * NZ)
    tiles = (2 * NX * 2 * NZ) // 2 + 1
    vmem = pl.BlockSpec(memory_space=pltpu.VMEM)
    anywhere = pl.BlockSpec(memory_space=pl.ANY)
    copies = 120

    def vm(*shape, dtype=BF16):
        return pltpu.VMEM(shape, dtype)

    rows = (NX, 2, 64, lanes)

    sums = [vm(NX, NZ, slab, 128), vm(NX, NZ, slab, 128), vm(NZ, slab, 128), vm(NZ, slab, 128)]
    return pl.pallas_call(
        layer_kernel,
        out_shape=(
            jax.ShapeDtypeStruct((tokens, 256), BF16),
            jax.ShapeDtypeStruct((slab, 128), F32),
            jax.ShapeDtypeStruct((slab, 64), F32),
            jax.ShapeDtypeStruct((slab, 64), F32),
            jax.ShapeDtypeStruct((slab, 128), F32),
        ),
        in_specs=[anywhere] * 6 + [vmem] * 2,
        out_specs=(vmem,) * 5,
        scratch_shapes=[
            vm(tokens, model), vm(tokens, model), vm(model, 256), vm(64, model), vm(64, model), vm(128, model),
            vm(NH, model // NH, 256), vm(model, tokens),
            vm(2, 64, lanes), vm(2, 64, lanes), vm(2, chunk, 128),
            vm(*rows), vm(*rows), vm(NZ, 2, chunk, 128), vm(NZ, 2, 144, chunk), vm(NX, 2, 128, 2 * lanes),
            vm(tiles, chunk, lanes), vm(tiles + 7, lanes, dtype=F32), vm(NX, 2, 16, lanes, dtype=F32),
            vm(8, lanes, dtype=F32), vm(8, lanes, dtype=F32), vm(*rows, dtype=F32), vm(*rows, dtype=F32),
            vm(NZ, 2, chunk, 128, dtype=F32),
            vm(*rows), vm(*rows), vm(64, lanes), vm(64, lanes), vm(*rows), vm(*rows), vm(64, lanes), vm(64, lanes),
            vm(128, tokens), vm(2, 128, tokens),
            vm(NZ, 2, chunk, 128), vm(NZ // 2, 2, chunk, 128), vm(NZ // 2, 2, chunk, 128),
            vm(chunk, 128), vm(chunk, 128),
        ] + sums + [
            vm(NX, NZ, slab, 128), vm(NZ, NX, slab, 128), vm(NX, slab, 128), vm(NX, slab, 128),
        ] + sums + [
            vm(NH, 2, 128, tokens), vm(256, tokens, dtype=F32),
            pltpu.SemaphoreType.DMA((copies,)),
            pltpu.SemaphoreType.DMA((copies,)),
            pltpu.SemaphoreType.DMA((6,)),
        ],
        compiler_params=pltpu.CompilerParams(
            collective_id=0, has_side_effects=True, vmem_limit_bytes=60 * 1024 * 1024
        ),
        name="layer",
    )(inputs, out_grad, w_query, w_key, w_value, w_output, cos_t, sin_t)


def hand_on_kernel(*refs):
    count = len(refs) // 2
    for source, target in zip(refs[:count], refs[count:]):
        target[...] = source[...]


def hand_on(arrays):
    vmem = pl.BlockSpec(memory_space=pltpu.VMEM)
    return pl.pallas_call(
        hand_on_kernel,
        out_shape=tuple(jax.ShapeDtypeStruct(array.shape, array.dtype) for array in arrays),
        in_specs=[vmem] * len(arrays),
        out_specs=(vmem,) * len(arrays),
        name="hand_on",
    )(*arrays)


def body(inputs, out_grad, w_query, w_key, w_value, w_output):
    tokens = inputs.shape[0]
    me = lax.axis_index("seq")
    positions = (me * tokens + jnp.arange(tokens, dtype=jnp.int32)).astype(F32)
    cos, sin = rotary(positions)
    results = layer(inputs, out_grad, w_query, w_key.T, w_value.T, w_output, cos.T, sin.T)
    *grads, grad_output = hand_on(results)
    return (*grads, grad_output.T)


def solution(mesh):
    placed = (
        P("seq", None),
        P("seq", None),
        P(None, "head"),
        P(None, "head"),
        P(None, "head"),
        P("head", None),
    )
    return jax.shard_map(
        body,
        mesh=mesh,
        in_specs=placed,
        out_specs=(
            P("seq", "head"),
            P("seq", "head"),
            P("seq", "head"),
            P("seq", "head"),
            P("head", "seq"),
        ),
        check_vma=False,
    )
```
